32 devices in a mesh: feat: 16 (over z, y, x), frame: 2 (over core).
Axes of the slice: x: 2, y: 2, z: 4, core: 2. Of those that a mesh axis runs over, the one named last changes fastest.
Arguments:
- frames: float32 [6144, 440], P(('frame', 'feat')), may hold values from -6 to 6
- labels: int32 [6144], P('frame'), may hold values from 0 to 146, as said below
- proj: float32 [440, 32768], P(None, 'feat'), may hold values from -1 to 1
- phase: float32 [32768], P('feat'), may hold values from 0 to 6.2832
- class_weights: float32 [32768, 147], P('feat'), may hold values from -40 to 40
- velocity: float32 [32768, 147], P('feat'), may hold values from -3 to 3
Outputs:
- weights_out: float32 [32768, 147], P('feat')
- velocity_out: float32 [32768, 147], P('feat')
The draws below stay inside these ranges and needn't reach their ends.
Inputs may be any that keep to these rules, and one draw needn't show every extreme that they name: labels come in runs of 4 to 12 consecutive frames that share one class (phone segments); neighbouring runs may share a class.
All inputs are finite; a program needn't handle non-finite values.
Results may differ from the reference program's by a relative error of at most 0.00011.
Values sent between devices are 32-bit elements; how exact they have to be, the bound alone decides.
No kernel may reach another device: no remote copies, remote signals or barrier semaphores. Data moves between devices by JAX's collectives and lax.ppermute only.
A program may use at most 128 MiB of HBM per device.

```python
import math
import jax
import jax.numpy as jnp
from jax import lax

IN_DIM = 440
CLASSES = 147
FEAT_DEV = 2048
ITERS = 2
FEATS = 32768
FRAMES = 6144


def segment_layout(key):
    seg_slots = FRAMES // 4 + 1
    seg_len = jax.random.randint(jax.random.fold_in(key, 5), (seg_slots,), 4, 13)
    starts = jnp.cumsum(seg_len) - seg_len
    marks = jnp.zeros((FRAMES,), jnp.int32).at[starts].add(1, mode='drop')
    seg_ids = jnp.cumsum(marks) - 1
    seg_class = jax.random.randint(jax.random.fold_in(key, 6), (seg_slots,), 0, CLASSES)
    return (seg_slots, seg_ids, seg_class)


def base_arrays(key):
    seg_slots, seg_ids, seg_class = segment_layout(key)
    key_shared, key_own, key_proj, key_phase, key_width = jax.random.split(jax.random.fold_in(key, 11), 5)
    shared = jax.random.normal(key_shared, (seg_slots, IN_DIM), jnp.float32)
    own = jax.random.normal(key_own, (FRAMES, IN_DIM), jnp.float32)
    top_width = 2.5
    frames = 2.5 * (math.sqrt(0.9) * shared[seg_ids] + math.sqrt(0.1) * own)
    frames = jnp.clip(frames, -6.0, 6.0)
    block_count = FEATS // FEAT_DEV
    jitter = jax.random.uniform(key_width, (block_count,), jnp.float32, 0.0, 1.0)
    position = (jnp.arange(block_count, dtype=jnp.float32) + jitter) / block_count
    widths = jnp.exp((1.0 - position) * math.log(top_width))
    widths = jnp.repeat(widths, FEAT_DEV)
    proj = jnp.clip(jax.random.normal(key_proj, (IN_DIM, FEATS), jnp.float32), -6.0, 6.0) / math.sqrt(IN_DIM)
    proj = jnp.clip(proj * widths[None, :], -1.0, 1.0)
    phase = jax.random.uniform(key_phase, (FEATS,), jnp.float32, 0.0, 6.2832)
    return (frames, proj, phase)


def draw_frames(key, part):
    return base_arrays(key)[0]


def draw_labels(key, part):
    seg_slots, seg_ids, seg_class = segment_layout(key)
    return seg_class[seg_ids].astype(jnp.int32)


def draw_proj(key, part):
    return base_arrays(key)[1]


def draw_phase(key, part):
    return base_arrays(key)[2]


def draw_class_weights(key, part):
    weights = 3.0 * jnp.clip(jax.random.normal(jax.random.fold_in(key, 23), (FEATS, CLASSES), jnp.float32), -6.0, 6.0)
    return weights


def level_of(key, extent, pieces, least, top_value):
    gain, own = 1.0, jax.random.fold_in(key, 6)
    for dim, blocks in pieces:
        draws = jnp.exp(jax.random.uniform(jax.random.fold_in(own, dim), (blocks,), jnp.float32, least / len(pieces), top_value / len(pieces)))
        gain = gain * jnp.repeat(draws, extent[dim] // blocks).reshape([-1 if axis == dim else 1 for axis in range(len(extent))])
    return gain


def bell_draw(key, dims, width, most, cuts=(), kind=jnp.bfloat16):
    drawn = jax.random.normal(key, dims, jnp.float32) * width
    if len(cuts) > 0:
        drawn = level_of(key, dims, cuts, -0.22, 0.18) * drawn
    return jnp.clip(drawn, min=-most, max=most).astype(kind)


def setup_inputs(seed: int = 0) -> dict:
    seeds = jax.random.split(jax.random.key(seed), 7)
    frames = draw_frames(jax.random.fold_in(seeds[6], 71), 0)
    labels = draw_labels(jax.random.fold_in(seeds[6], 71), 0)
    proj = draw_proj(jax.random.fold_in(seeds[6], 71), 0)
    phase = draw_phase(jax.random.fold_in(seeds[6], 71), 0)
    class_weights = draw_class_weights(jax.random.fold_in(seeds[6], 71), 0)
    velocity = bell_draw(seeds[5], (FEATS, CLASSES), 0.5, 3.0, ((0, 16),), jnp.float32)
    return dict(frames=frames, labels=labels, proj=proj, phase=phase, class_weights=class_weights, velocity=velocity)


MOMENTUM = 0.9
STEP_RATE = 0.05
EPSILON = 1e-06

def featurize(frame_rows, proj_block, phase_block):
    angles = jnp.dot(frame_rows, proj_block, precision=lax.Precision.HIGHEST, preferred_element_type=jnp.float32)
    return math.sqrt(2.0 / FEATS) * jnp.cos(angles + phase_block[None, :])

def reference(frames, labels, proj, phase, class_weights, velocity):
    block_width = math.gcd(FEATS, 4096)
    block_count = FEATS // block_width
    onehot = (labels[:, None] == jnp.arange(CLASSES, dtype=jnp.int32)[None, :]).astype(jnp.float32)
    proj_blocks = proj.reshape(IN_DIM, block_count, block_width).transpose(1, 0, 2)
    phase_blocks = phase.reshape(block_count, block_width)
    weights_now = class_weights
    velocity_now = velocity
    for iteration in range(ITERS):
        advance = weights_now + MOMENTUM * velocity_now
        look_blocks = advance.reshape(block_count, block_width, CLASSES)

        def add_scores(scores, inputs_block):
            proj_block, phase_block, look_block = inputs_block
            features = featurize(frames, proj_block, phase_block)
            return (scores + jnp.dot(features, look_block, precision=lax.Precision.HIGHEST, preferred_element_type=jnp.float32), None)
        scores, unused = lax.scan(add_scores, jnp.zeros((FRAMES, CLASSES), jnp.float32), (proj_blocks, phase_blocks, look_blocks))
        row_max = lax.optimization_barrier(jnp.max(scores, axis=1, keepdims=True))
        exponent = jnp.exp(scores - row_max)
        probability = exponent / lax.optimization_barrier(jnp.sum(exponent, axis=1, keepdims=True))
        residual = probability - onehot

        def grad_block(inputs_block):
            proj_block, phase_block = inputs_block
            features = featurize(frames, proj_block, phase_block)
            return lax.dot_general(features, residual, (((0,), (0,)), ((), ())), precision=lax.Precision.HIGHEST, preferred_element_type=jnp.float32)
        gradient = lax.map(grad_block, (proj_blocks, phase_blocks)).reshape(FEATS, CLASSES)
        grad_rms = jnp.sqrt(jnp.sum(gradient * gradient) / (FEATS * CLASSES) + EPSILON)
        velocity_now = MOMENTUM * velocity_now - STEP_RATE * gradient / grad_rms
        weights_now = weights_now + velocity_now
    return (weights_now, velocity_now)
```

```python
import functools
import math

import jax
import jax.numpy as jnp
from jax import lax
from jax.experimental import pallas as pl
from jax.experimental.pallas import tpu as pltpu
from jax.sharding import PartitionSpec as P

ITERS = 2


MOMENTUM = 0.9
STEP_RATE = 0.05
EPSILON = 1e-06

BF16 = jnp.bfloat16
F32 = jnp.float32
NN = (((1,), (0,)), ((), ()))
NT = (((1,), (1,)), ((), ()))
MAGIC = 12582912.0
TURN = 1.0 / (2.0 * math.pi)
COS = (
    0.9999992107823203,
    -19.73898035576386,
    64.92865742102978,
    -85.2716215342655,
    58.790492119989025,
    -21.071105627426505,
)
VMEM_LIMIT = 48 * 2**20


def split(value):
    high = value.astype(BF16)
    return high, (value - high.astype(F32)).astype(BF16)


def dot(left, right, dims):
    return lax.dot_general(left, right, dims, preferred_element_type=F32)


def cos_turns(turns):
    rest = turns - ((turns + MAGIC) - MAGIC)
    square = rest * rest
    total = jnp.float32(COS[-1])
    for factor in COS[-2::-1]:
        total = total * square + jnp.float32(factor)
    return total


def pad_rows(count):
    return -(-count // 8) * 8


def features_kernel(frames, proj, phase, look, high, low, scores, proj_parts, look_parts, *, width):
    classes = look.shape[0]
    rows = scores.shape[0]

    @pl.when(pl.program_id(0) == 0)
    def _():
        proj_parts[0], proj_parts[1] = split(proj[...] * F32(TURN))
        look_parts[...] = jnp.zeros(look_parts.shape, BF16)
        look_parts[0:classes], look_parts[rows : rows + classes] = split(look[...])

    x_high, x_low = split(frames[...])
    total = jnp.zeros(scores.shape, F32)
    for start in range(0, proj.shape[1], width):
        part = slice(start, start + width)
        turns = (
            dot(x_high, proj_parts[0, :, part], NN)
            + dot(x_high, proj_parts[1, :, part], NN)
            + dot(x_low, proj_parts[0, :, part], NN)
        )
        f_high, f_low = split(cos_turns(turns + phase[:, part] * F32(TURN)))
        high[:, part] = f_high
        low[:, part] = f_low
        both = dot(look_parts[:, part], f_high, NT)
        total += both[:rows] + both[rows:] + dot(look_parts[:rows, part], f_low, NT)
    scores[...] = total


def features_call(frames, proj, phase, look, tile, width):
    count, depth = frames.shape
    feats = proj.shape[1]
    classes = look.shape[0]
    rows = pad_rows(classes)
    return pl.pallas_call(
        functools.partial(features_kernel, width=width),
        grid=(count // tile,),
        in_specs=[
            pl.BlockSpec((tile, depth), lambda i: (i, 0)),
            pl.BlockSpec((depth, feats), lambda i: (0, 0)),
            pl.BlockSpec((1, feats), lambda i: (0, 0)),
            pl.BlockSpec((classes, feats), lambda i: (0, 0)),
        ],
        out_specs=[
            pl.BlockSpec((tile, feats), lambda i: (i, 0)),
            pl.BlockSpec((tile, feats), lambda i: (i, 0)),
            pl.BlockSpec((rows, tile), lambda i: (0, i)),
        ],
        out_shape=[
            jax.ShapeDtypeStruct((count, feats), BF16),
            jax.ShapeDtypeStruct((count, feats), BF16),
            jax.ShapeDtypeStruct((rows, count), F32),
        ],
        scratch_shapes=[pltpu.VMEM((2, depth, feats), BF16), pltpu.VMEM((2 * rows, feats), BF16)],
        compiler_params=pltpu.CompilerParams(vmem_limit_bytes=VMEM_LIMIT),
        name="features",
    )(frames, proj, phase, look)


def scores_kernel(look, high, low, scores, look_parts):
    classes = look.shape[0]
    rows = scores.shape[0]

    @pl.when(pl.program_id(0) == 0)
    def _():
        look_parts[...] = jnp.zeros(look_parts.shape, BF16)
        look_parts[0:classes], look_parts[rows : rows + classes] = split(look[...])

    both = dot(look_parts[...], high[...], NT)
    scores[...] = both[:rows] + both[rows:] + dot(look_parts[:rows], low[...], NT)


def scores_call(look, high, low, tile):
    count, feats = high.shape
    classes = look.shape[0]
    rows = pad_rows(classes)
    return pl.pallas_call(
        scores_kernel,
        grid=(count // tile,),
        in_specs=[
            pl.BlockSpec((classes, feats), lambda i: (0, 0)),
            pl.BlockSpec((tile, feats), lambda i: (i, 0)),
            pl.BlockSpec((tile, feats), lambda i: (i, 0)),
        ],
        out_specs=pl.BlockSpec((rows, tile), lambda i: (0, i)),
        out_shape=jax.ShapeDtypeStruct((rows, count), F32),
        scratch_shapes=[pltpu.VMEM((2 * rows, feats), BF16)],
        compiler_params=pltpu.CompilerParams(vmem_limit_bytes=VMEM_LIMIT),
        name="scores",
    )(look, high, low)


def gradient_kernel(residual, high, low, gradient, *, width):
    rows = gradient.shape[0]

    @pl.when(pl.program_id(0) == 0)
    def _():
        gradient[...] = jnp.zeros(gradient.shape, F32)

    r_high, r_low = split(residual[...])
    r_both = jnp.concatenate([r_high, r_low], axis=0)
    for start in range(0, gradient.shape[1], width):
        part = slice(start, start + width)
        both = dot(r_both, high[:, part], NN)
        gradient[:, part] += both[:rows] + both[rows:] + dot(r_high, low[:, part], NN)


def gradient_call(residual, high, low, tile, width):
    count, feats = high.shape
    rows = residual.shape[0]
    return pl.pallas_call(
        functools.partial(gradient_kernel, width=width),
        grid=(count // tile,),
        in_specs=[
            pl.BlockSpec((rows, tile), lambda i: (0, i)),
            pl.BlockSpec((tile, feats), lambda i: (i, 0)),
            pl.BlockSpec((tile, feats), lambda i: (i, 0)),
        ],
        out_specs=pl.BlockSpec((rows, feats), lambda i: (0, 0)),
        out_shape=jax.ShapeDtypeStruct((rows, feats), F32),
        compiler_params=pltpu.CompilerParams(vmem_limit_bytes=VMEM_LIMIT),
        name="gradient",
    )(residual, high, low)


def tile_of(count, most):
    return max(t for t in range(128, most + 1, 128) if count % t == 0)


def residual_of(scores, labels, classes, scale):
    row = lax.broadcasted_iota(jnp.int32, scores.shape, 0)
    scores = jnp.where(row < classes, scores * scale, -jnp.inf)
    exponent = jnp.exp(scores - jnp.max(scores, axis=0, keepdims=True))
    probability = exponent / jnp.sum(exponent, axis=0, keepdims=True)
    return probability - (row == labels[None, :]).astype(F32)


def on_device(frames, labels, proj, phase, class_weights, velocity):
    feat_count = lax.axis_size("feat") * proj.shape[1]
    classes = class_weights.shape[1]
    feat_scale = math.sqrt(2.0 / feat_count)
    count_all = feat_count * classes
    gathered = lax.all_gather(frames, "feat", axis=0, tiled=True)
    tile = tile_of(gathered.shape[0], 512)
    weights_now = class_weights.T
    velocity_now = velocity.T
    for iteration in range(ITERS):
        advance = weights_now + MOMENTUM * velocity_now
        if iteration == 0:
            high, low, partial_value = features_call(gathered, proj, phase[None, :], advance, tile, 512)
        else:
            partial_value = scores_call(advance, high, low, tile)
        scores = lax.psum(partial_value, "feat")
        residual = residual_of(scores, labels, classes, feat_scale)
        grad_local = gradient_call(residual, high, low, tile, 512)[:classes] * feat_scale
        others = lax.axis_size("frame")
        gradient = grad_local
        moved = grad_local
        for _ in range(others - 1):
            moved = lax.ppermute(moved, "frame", [(i, (i + 1) % others) for i in range(others)])
            gradient = gradient + moved
        square_sum = lax.psum(jnp.sum(gradient * gradient), "feat")
        grad_rms = jnp.sqrt(square_sum / count_all + EPSILON)
        velocity_now = MOMENTUM * velocity_now - STEP_RATE * gradient / grad_rms
        weights_now = weights_now + velocity_now
    return (weights_now.T, velocity_now.T)


def solution(mesh):
    return jax.shard_map(
        on_device,
        mesh=mesh,
        in_specs=(
            P(("frame", "feat"), None),
            P("frame"),
            P(None, "feat"),
            P("feat"),
            P("feat", None),
            P("feat", None),
        ),
        out_specs=(P("feat", None), P("feat", None)),
        check_vma=False,
    )
```

```python
import functools
import math

import jax
import jax.numpy as jnp
from jax import lax
from jax.experimental import pallas as pl
from jax.experimental.pallas import tpu as pltpu
from jax.sharding import PartitionSpec as P

ITERS = 2


MOMENTUM = 0.9
STEP_RATE = 0.05
EPSILON = 1e-06

BF16 = jnp.bfloat16
F32 = jnp.float32
NN = (((1,), (0,)), ((), ()))
NT = (((1,), (1,)), ((), ()))
MAGIC = 12582912.0
TURN = 1.0 / (2.0 * math.pi)
COS = (
    0.9999992107823203,
    -19.73898035576386,
    64.92865742102978,
    -85.2716215342655,
    58.790492119989025,
    -21.071105627426505,
)
VMEM_LIMIT = 48 * 2**20
LANES = 128
GROUP = 4


def split(value):
    high = value.astype(BF16)
    return high, (value - high.astype(F32)).astype(BF16)


def split_array(value):
    high = lax.reduce_precision(value, exponent_bits=8, mantissa_bits=7)
    return high.astype(BF16), (value - high).astype(BF16)


def dot(left, right, dims):
    return lax.dot_general(left, right, dims, preferred_element_type=F32)


def cos_turns(turns):
    rest = turns - ((turns + MAGIC) - MAGIC)
    square = rest * rest
    total = jnp.float32(COS[-1])
    for factor in COS[-2::-1]:
        total = total * square + jnp.float32(factor)
    return total


def pad_rows(count):
    return -(-count // 8) * 8


def fold_plan(rows, columns):
    rest = columns % LANES
    if rest == 0 or LANES % rest or columns > 2 * LANES:
        return [((0, rows), (0, columns), 0, 0)], (rows, columns)
    whole = columns - rest
    pieces = LANES // rest
    height = pad_rows(-(-rows // pieces))
    moves = [((0, rows), (0, whole), 0, 0)] if whole else []
    base = rows if whole else 0
    for piece in range(pieces):
        top, end = piece * height, min((piece + 1) * height, rows)
        if top < end:
            moves.append(((top, end), (whole, columns), base, piece * rest))
    return moves, (base + height, LANES)


def pack_into(ref, value):
    moves, shape = fold_plan(*value.shape)
    if len(moves) > 1:
        ref[shape[0] - 8 : shape[0], :] = jnp.zeros((8, shape[1]), F32)
    for (top, end), (left, right), row, lane in moves:
        ref[row : row + end - top, lane : lane + right - left] = value[top:end, left:right]


def unpack_into(ref, start, packed, columns):
    moves, _ = fold_plan(ref.shape[0], columns)
    for (top, end), (left, right), row, lane in moves:
        ref[top:end, start + left : start + right] = packed[row : row + end - top, lane : lane + right - left]


def tree_edges(count):
    bits = count.bit_length() - 1
    assert count == 1 << bits
    loads = [0] * bits
    edges = []
    for level in range(1, bits + 1):
        nodes = [n for n in range(count) if n.bit_count() == level]
        for node in sorted(nodes, key=lambda n: -n):
            choices = [b for b in range(bits) if node >> b & 1]
            if len(choices) > 1 and choices[-1] == bits - 1:
                choices = choices[:-1]
            bit = min(choices, key=lambda b: loads[b])
            loads[bit] += 1
            edges.append((bit, node ^ (1 << bit), node))
    return edges


def swap(value, axis, bit):
    count = lax.axis_size(axis)
    return lax.ppermute(value, axis, [(i, i ^ (1 << bit)) for i in range(count)])


def spread(block, axis):
    known = {0: block}
    for bit, parent, child in tree_edges(lax.axis_size(axis)):
        known[child] = swap(known[parent], axis, bit)
    return known


def gather_sum(blocks, axis):
    total = dict(blocks)
    for bit, parent, child in reversed(tree_edges(lax.axis_size(axis))):
        total[parent] = total[parent] + swap(total[child], axis, bit)
    return total[0]


def sum_over(value, axis):
    for bit in range(lax.axis_size(axis).bit_length() - 1):
        value = value + swap(value, axis, bit)
    return value


def groups_of(axis):
    order = [0] + [child for _, _, child in tree_edges(lax.axis_size(axis))]
    return [order[i : i + GROUP] for i in range(0, len(order), GROUP)]


def features_kernel(*refs, blocks):
    frames, refs = refs[:blocks], refs[blocks:]
    p_high, p_low, phase, look, look_high, high, low = refs[:7]
    scores, (x_parts, total) = refs[7 : 7 + blocks], refs[7 + blocks :]
    columns = frames[0].shape[0]
    rows = look_high.shape[0]
    step = pl.program_id(0)

    @pl.when(step == 0)
    def _():
        for j in range(blocks):
            part = slice(j * columns, (j + 1) * columns)
            x_parts[0, part], x_parts[1, part] = split(frames[j][...])
        total[...] = jnp.zeros(total.shape, F32)

    turns = (
        dot(x_parts[0], p_high[...], NN) + dot(x_parts[0], p_low[...], NN) + dot(x_parts[1], p_high[...], NN)
    )
    f_high, f_low = split(cos_turns(turns + phase[...]))
    high[...] = f_high
    low[...] = f_low
    both = dot(look[...], f_high, NT)
    total[...] += both[:rows] + both[rows:] + dot(look_high[...], f_low, NT)

    @pl.when(step == pl.num_programs(0) - 1)
    def _():
        for j in range(blocks):
            pack_into(scores[j], total[:, j * columns : (j + 1) * columns])


def features_call(frames, proj, phase, look, width):
    blocks = len(frames)
    columns, depth = frames[0].shape
    count = blocks * columns
    feats = proj[0].shape[1]
    rows = look[1].shape[0]
    packed = fold_plan(rows, columns)[1]
    return pl.pallas_call(
        functools.partial(features_kernel, blocks=blocks),
        grid=(feats // width,),
        in_specs=[pl.BlockSpec((columns, depth), lambda i: (0, 0))] * blocks
        + [pl.BlockSpec((depth, width), lambda i: (0, i))] * 2
        + [
            pl.BlockSpec((1, width), lambda i: (0, i)),
            pl.BlockSpec((2 * rows, width), lambda i: (0, i)),
            pl.BlockSpec((rows, width), lambda i: (0, i)),
        ],
        out_specs=[pl.BlockSpec((count, width), lambda i: (0, i))] * 2
        + [pl.BlockSpec(packed, lambda i: (0, 0))] * blocks,
        out_shape=[jax.ShapeDtypeStruct((count, feats), BF16)] * 2
        + [jax.ShapeDtypeStruct(packed, F32)] * blocks,
        scratch_shapes=[pltpu.VMEM((2, count, depth), BF16), pltpu.VMEM((rows, count), F32)],
        compiler_params=pltpu.CompilerParams(vmem_limit_bytes=VMEM_LIMIT),
        cost_estimate=pl.CostEstimate(
            flops=6 * count * feats * (depth + rows), bytes_accessed=4 * count * feats, transcendentals=0
        ),
        name="features",
    )(*frames, *proj, phase, *look)


def scores_kernel(look, look_high, high, low, *refs, blocks):
    scores, total = refs[:blocks], refs[blocks]
    rows = look_high.shape[0]
    columns = total.shape[1] // blocks
    step = pl.program_id(0)

    @pl.when(step == 0)
    def _():
        total[...] = jnp.zeros(total.shape, F32)

    both = dot(look[...], high[...], NT)
    total[...] += both[:rows] + both[rows:] + dot(look_high[...], low[...], NT)

    @pl.when(step == pl.num_programs(0) - 1)
    def _():
        for j in range(blocks):
            pack_into(scores[j], total[:, j * columns : (j + 1) * columns])


def scores_call(look, high, low, blocks, width):
    count, feats = high.shape
    rows = look[1].shape[0]
    packed = fold_plan(rows, count // blocks)[1]
    return pl.pallas_call(
        functools.partial(scores_kernel, blocks=blocks),
        grid=(feats // width,),
        in_specs=[
            pl.BlockSpec((2 * rows, width), lambda i: (0, i)),
            pl.BlockSpec((rows, width), lambda i: (0, i)),
            pl.BlockSpec((count, width), lambda i: (0, i)),
            pl.BlockSpec((count, width), lambda i: (0, i)),
        ],
        out_specs=[pl.BlockSpec(packed, lambda i: (0, 0))] * blocks,
        out_shape=[jax.ShapeDtypeStruct(packed, F32)] * blocks,
        scratch_shapes=[pltpu.VMEM((rows, count), F32)],
        compiler_params=pltpu.CompilerParams(vmem_limit_bytes=VMEM_LIMIT),
        cost_estimate=pl.CostEstimate(
            flops=6 * count * feats * rows, bytes_accessed=4 * count * feats, transcendentals=0
        ),
        name="scores",
    )(*look, high, low)


def gradient_kernel(*refs, blocks, columns, first):
    residual, refs = refs[:blocks], refs[blocks:]
    if first:
        high, low, gradient, spread_out, parts = refs
    else:
        high, low, before, gradient, spread_out, parts = refs
    rows = gradient.shape[0]

    @pl.when(pl.program_id(0) == 0)
    def _():
        for j in range(blocks):
            unpack_into(spread_out, j * columns, residual[j], columns)
        r_high, r_low = split(spread_out[...])
        parts[...] = jnp.concatenate([r_high, r_low], axis=0)

    both = dot(parts[...], high[...], NN)
    value = both[:rows] + both[rows:] + dot(parts[:rows], low[...], NN)
    gradient[...] = value if first else before[...] + value


def gradient_call(residual, high, low, before, columns, rows, width):
    blocks = len(residual)
    count, feats = high.shape
    first = before is None
    return pl.pallas_call(
        functools.partial(gradient_kernel, blocks=blocks, columns=columns, first=first),
        grid=(feats // width,),
        in_specs=[pl.BlockSpec(residual[0].shape, lambda i: (0, 0))] * blocks
        + [pl.BlockSpec((count, width), lambda i: (0, i))] * 2
        + [pl.BlockSpec((rows, width), lambda i: (0, i))] * (not first),
        out_specs=pl.BlockSpec((rows, width), lambda i: (0, i)),
        out_shape=jax.ShapeDtypeStruct((rows, feats), F32),
        input_output_aliases={} if first else {blocks + 2: 0},
        scratch_shapes=[pltpu.VMEM((rows, count), F32), pltpu.VMEM((2 * rows, count), BF16)],
        compiler_params=pltpu.CompilerParams(vmem_limit_bytes=VMEM_LIMIT),
        cost_estimate=pl.CostEstimate(
            flops=6 * count * feats * rows, bytes_accessed=4 * count * feats, transcendentals=0
        ),
        name="gradient",
    )(*residual, high, low, *([] if first else [before]))


def residual_kernel(scores, labels, residual, plain, *, classes, scale):
    columns = plain.shape[1]
    unpack_into(plain, 0, scores, columns)
    row = lax.broadcasted_iota(jnp.int32, plain.shape, 0)
    value = jnp.where(row < classes, plain[...] * F32(scale), -jnp.inf)
    exponent = jnp.exp(value - jnp.max(value, axis=0, keepdims=True))
    probability = exponent / jnp.sum(exponent, axis=0, keepdims=True)
    pack_into(residual, probability - (row == labels[...]).astype(F32))


def residual_call(scores, labels, classes, scale):
    rows, columns = pad_rows(classes), labels.shape[0]
    return pl.pallas_call(
        functools.partial(residual_kernel, classes=classes, scale=scale),
        out_shape=jax.ShapeDtypeStruct(scores.shape, F32),
        scratch_shapes=[pltpu.VMEM((rows, columns), F32)],
        name="residual",
    )(scores, labels[None, :])


def look_parts(advance):
    rows = pad_rows(advance.shape[0])
    high, low = split_array(jnp.pad(advance, ((0, rows - advance.shape[0]), (0, 0))))
    return jnp.concatenate([high, low], axis=0), high


def on_device(frames, labels, proj, phase, class_weights, velocity):
    feat_count = lax.axis_size("feat") * proj.shape[1]
    classes = class_weights.shape[1]
    feat_scale = math.sqrt(2.0 / feat_count)
    count_all = feat_count * classes
    columns = frames.shape[0]
    rows = pad_rows(classes)
    groups = groups_of("feat")
    labels_own = lax.dynamic_slice(labels, (lax.axis_index("feat") * columns,), (columns,))
    known = spread(frames, "feat")
    proj_parts = split_array(proj * F32(TURN))
    phase_turns = (phase * F32(TURN))[None, :]
    weights_now = class_weights.T
    velocity_now = velocity.T
    parts = [None] * len(groups)
    for iteration in range(ITERS):
        look = look_parts(weights_now + MOMENTUM * velocity_now)
        partial_value = {}
        for g in range(len(groups)) if iteration == 0 else reversed(range(len(groups))):
            group = groups[g]
            if iteration == 0:
                high, low, *sums = features_call([known[j] for j in group], proj_parts, phase_turns, look, 512)
                parts[g] = high, low
            else:
                sums = scores_call(look, *parts[g], len(group), 512)
            partial_value.update(zip(group, sums))
        scores = gather_sum(partial_value, "feat")
        residual = spread(residual_call(scores, labels_own, classes, feat_scale), "feat")
        gradient = None
        for g, group in enumerate(groups):
            gradient = gradient_call([residual[j] for j in group], *parts[g], gradient, columns, rows, 512)
        grad_local = gradient[:classes] * feat_scale
        gradient = sum_over(grad_local, "frame")
        square_sum = sum_over(jnp.sum(gradient * gradient, keepdims=True), "feat")
        grad_rms = jnp.sqrt(square_sum / count_all + EPSILON)
        velocity_now = MOMENTUM * velocity_now - STEP_RATE * gradient / grad_rms
        weights_now = weights_now + velocity_now
    return (weights_now.T, velocity_now.T)


def solution(mesh):
    return jax.shard_map(
        on_device,
        mesh=mesh,
        in_specs=(
            P(("frame", "feat"), None),
            P("frame"),
            P(None, "feat"),
            P("feat"),
            P("feat", None),
            P("feat", None),
        ),
        out_specs=(P("feat", None), P("feat", None)),
        check_vma=False,
    )
```

```python
import functools
import math

import jax
import jax.numpy as jnp
from jax import lax
from jax.experimental import pallas as pl
from jax.experimental.pallas import tpu as pltpu
from jax.sharding import PartitionSpec as P

ITERS = 2


MOMENTUM = 0.9
STEP_RATE = 0.05
EPSILON = 1e-06

BF16 = jnp.bfloat16
F32 = jnp.float32
NN = (((1,), (0,)), ((), ()))
NT = (((1,), (1,)), ((), ()))
MAGIC = 12582912.0
TURN = 1.0 / (2.0 * math.pi)
COS = (
    0.9999992107823203,
    -19.73898035576386,
    64.92865742102978,
    -85.2716215342655,
    58.790492119989025,
    -21.071105627426505,
)
VMEM_FEATURES = 18 * 2**20
VMEM_PRODUCTS = 16 * 2**20
VMEM_RESIDUAL = 8 * 2**20


def split(value):
    high = value.astype(BF16)
    return high, (value - high.astype(F32)).astype(BF16)


def split_array(value):
    high = lax.reduce_precision(value, exponent_bits=8, mantissa_bits=7)
    return high.astype(BF16), (value - high).astype(BF16)


def dot(left, right, dims):
    return lax.dot_general(left, right, dims, preferred_element_type=F32)


def cos_turns(turns):
    rest = turns - ((turns + MAGIC) - MAGIC)
    square = rest * rest
    total = jnp.float32(COS[-1])
    for factor in COS[-2::-1]:
        total = total * square + jnp.float32(factor)
    return total


def pad_rows(count):
    return -(-count // 8) * 8


def tree_edges(bits):
    loads, free, arrival, edges = [0] * bits, [0] * bits, {0: 0}, []
    for level in range(1, bits + 1):
        nodes = [n for n in range(1 << bits) if n.bit_count() == level]
        for node in sorted(nodes, key=lambda n: -n):
            choices = [b for b in range(bits) if node >> b & 1]
            if len(choices) > 1 and choices[-1] == bits - 1:
                choices = choices[:-1]
            bit = min(choices, key=lambda b: loads[b])
            loads[bit] += 1
            edges.append((bit, node ^ (1 << bit), node))
    ordered = []
    while edges:
        ready = [e for e in edges if e[1] in arrival]
        cost = lambda e: max(arrival[e[1]], free[e[0]]) + 1 + (e[0] == bits - 1)
        edge = min(ready, key=lambda e: (cost(e), -sum(e[2] & c[2] == e[2] for c in edges)))
        arrival[edge[2]] = free[edge[0]] = cost(edge)
        edges.remove(edge)
        ordered.append(edge)
    return ordered, arrival


def swap(value, axis, bit):
    count = lax.axis_size(axis)
    return lax.ppermute(value, axis, [(i, i ^ (1 << bit)) for i in range(count)])


def spread(item, axis, bits):
    known = {0: item}
    for bit, parent, child in tree_edges(len(bits))[0]:
        known[child] = swap(known[parent], axis, bits[bit])
    return known


def gather_sum(items, axis, bits):
    total = dict(items)
    for bit, parent, child in reversed(tree_edges(len(bits))[0]):
        total[parent] = total[parent] + swap(total[child], axis, bits[bit])
    return total[0]


def sum_over(value, axis):
    count = lax.axis_size(axis)
    bits = count.bit_length() - 1
    for low in range(0, bits, 2):
        steps = [1 << low] if low + 1 == bits else [1 << low, 2 << low, 3 << low]
        value = sum((lax.ppermute(value, axis, [(i, i ^ s) for i in range(count)]) for s in steps), value)
    return value


def units_of(axis):
    bits = lax.axis_size(axis).bit_length() - 1
    pair = bits - 2
    others = [b for b in range(bits) if b != pair]
    arrival = tree_edges(bits)[1]
    blocks = []
    for unit in range(1 << len(others)):
        first = sum((unit >> k & 1) << b for k, b in enumerate(others))
        blocks.append((first, first ^ (1 << pair)))
    order = sorted(range(len(blocks)), key=lambda u: (max(arrival[j] for j in blocks[u]), -u))
    return pair, others, blocks, [order[:1]] + [order[i : i + 2] for i in range(1, len(order), 2)]


def features_kernel(*refs, blocks):
    frames, refs = refs[:blocks], refs[blocks:]
    p_high, p_low, phase, look, look_high, _, high, low = refs[:8]
    scores, (x_parts, total) = refs[8:-2], refs[-2:]
    columns = frames[0].shape[0]
    rows = look_high.shape[0]
    step = pl.program_id(0)

    @pl.when(step == 0)
    def _():
        for j in range(blocks):
            part = slice(j * columns, (j + 1) * columns)
            x_parts[0, part], x_parts[1, part] = split(frames[j][...])
        total[...] = jnp.zeros(total.shape, F32)

    turns = (
        dot(x_parts[0], p_high[...], NN) + dot(x_parts[0], p_low[...], NN) + dot(x_parts[1], p_high[...], NN)
    )
    f_high, f_low = split(cos_turns(turns + phase[...]))
    high[...] = f_high
    low[...] = f_low
    both = dot(look[...], f_high, NT)
    total[...] += both[:rows] + both[rows:] + dot(look_high[...], f_low, NT)

    @pl.when(step == pl.num_programs(0) - 1)
    def _():
        width = 2 * columns
        for j in range(blocks // 2):
            scores[j][...] = total[:, j * width : (j + 1) * width]


def features_call(frames, proj, phase, look, after, width):
    blocks = len(frames)
    columns, depth = frames[0].shape
    count = blocks * columns
    feats = proj[0].shape[1]
    rows = look[1].shape[0]
    unit = (rows, 2 * columns)
    return pl.pallas_call(
        functools.partial(features_kernel, blocks=blocks),
        grid=(feats // width,),
        in_specs=[pl.BlockSpec((columns, depth), lambda i: (0, 0))] * blocks
        + [pl.BlockSpec((depth, width), lambda i: (0, i))] * 2
        + [
            pl.BlockSpec((1, width), lambda i: (0, i)),
            pl.BlockSpec((2 * rows, width), lambda i: (0, i)),
            pl.BlockSpec((rows, width), lambda i: (0, i)),
            pl.BlockSpec(memory_space=pl.ANY),
        ],
        out_specs=[pl.BlockSpec((count, width), lambda i: (0, i))] * 2
        + [pl.BlockSpec(unit, lambda i: (0, 0))] * (blocks // 2),
        out_shape=[jax.ShapeDtypeStruct((count, feats), BF16)] * 2
        + [jax.ShapeDtypeStruct(unit, F32)] * (blocks // 2),
        scratch_shapes=[pltpu.VMEM((2, count, depth), BF16), pltpu.VMEM((rows, count), F32)],
        compiler_params=pltpu.CompilerParams(vmem_limit_bytes=VMEM_FEATURES),
        cost_estimate=pl.CostEstimate(
            flops=6 * count * feats * (depth + rows), bytes_accessed=4 * count * feats, transcendentals=0
        ),
        name="features",
    )(*frames, *proj, phase, *look, after)


def scores_kernel(look, look_high, high, low, _, *refs):
    scores, total = refs[:-1], refs[-1]
    rows = look_high.shape[0]
    step = pl.program_id(0)

    @pl.when(step == 0)
    def _():
        total[...] = jnp.zeros(total.shape, F32)

    both = dot(look[...], high[...], NT)
    total[...] += both[:rows] + both[rows:] + dot(look_high[...], low[...], NT)

    @pl.when(step == pl.num_programs(0) - 1)
    def _():
        width = total.shape[1] // len(scores)
        for j, out in enumerate(scores):
            out[...] = total[:, j * width : (j + 1) * width]


def scores_call(look, high, low, after, units, width):
    count, feats = high.shape
    rows = look[1].shape[0]
    unit = (rows, count // units)
    return pl.pallas_call(
        scores_kernel,
        grid=(feats // width,),
        in_specs=[
            pl.BlockSpec((2 * rows, width), lambda i: (0, i)),
            pl.BlockSpec((rows, width), lambda i: (0, i)),
            pl.BlockSpec((count, width), lambda i: (0, i)),
            pl.BlockSpec((count, width), lambda i: (0, i)),
            pl.BlockSpec(memory_space=pl.ANY),
        ],
        out_specs=[pl.BlockSpec(unit, lambda i: (0, 0))] * units,
        out_shape=[jax.ShapeDtypeStruct(unit, F32)] * units,
        scratch_shapes=[pltpu.VMEM((rows, count), F32)],
        compiler_params=pltpu.CompilerParams(vmem_limit_bytes=VMEM_PRODUCTS),
        cost_estimate=pl.CostEstimate(
            flops=6 * count * feats * rows, bytes_accessed=4 * count * feats, transcendentals=0
        ),
        name="scores",
    )(*look, high, low, after)


def gradient_kernel(*refs, units, first):
    residual, refs = refs[:units], refs[units:]
    if first:
        high, low, gradient, parts = refs
    else:
        high, low, before, gradient, parts = refs
    rows, width = residual[0].shape

    @pl.when(pl.program_id(0) == 0)
    def _():
        for j in range(units):
            r_high, r_low = split(residual[j][...])
            parts[:, j * width : (j + 1) * width] = jnp.concatenate([r_high, r_low], axis=0)

    both = dot(parts[...], high[...], NN)
    value = both[:rows] + both[rows:] + dot(parts[:rows], low[...], NN)
    gradient[...] = value if first else before[...] + value


def gradient_call(residual, high, low, before, width):
    units = len(residual)
    rows = residual[0].shape[0]
    count, feats = high.shape
    first = before is None
    return pl.pallas_call(
        functools.partial(gradient_kernel, units=units, first=first),
        grid=(feats // width,),
        in_specs=[pl.BlockSpec(residual[0].shape, lambda i: (0, 0))] * units
        + [pl.BlockSpec((count, width), lambda i: (0, i))] * 2
        + [pl.BlockSpec((rows, width), lambda i: (0, i))] * (not first),
        out_specs=pl.BlockSpec((rows, width), lambda i: (0, i)),
        out_shape=jax.ShapeDtypeStruct((rows, feats), F32),
        input_output_aliases={} if first else {units + 2: 0},
        scratch_shapes=[pltpu.VMEM((2 * rows, count), BF16)],
        compiler_params=pltpu.CompilerParams(vmem_limit_bytes=VMEM_PRODUCTS),
        cost_estimate=pl.CostEstimate(
            flops=6 * count * feats * rows, bytes_accessed=4 * count * feats, transcendentals=0
        ),
        name="gradient",
    )(*residual, high, low, *([] if first else [before]))


def residual_kernel(mine, theirs, labels, residual, *, classes, scale):
    half = mine.shape[1] // 2
    row = lax.broadcasted_iota(jnp.int32, mine.shape, 0)
    turned = jnp.concatenate([theirs[:, half:], theirs[:, :half]], axis=1)
    value = jnp.where(row < classes, (mine[...] + turned) * F32(scale), -jnp.inf)
    exponent = jnp.exp(value - jnp.max(value, axis=0, keepdims=True))
    probability = exponent / jnp.sum(exponent, axis=0, keepdims=True)
    residual[...] = probability - (row == labels[...]).astype(F32)


def residual_call(mine, theirs, labels, classes, scale):
    return pl.pallas_call(
        functools.partial(residual_kernel, classes=classes, scale=scale),
        out_shape=jax.ShapeDtypeStruct(mine.shape, F32),
        compiler_params=pltpu.CompilerParams(vmem_limit_bytes=VMEM_RESIDUAL),
        name="residual",
    )(mine, theirs, labels)


def look_parts(advance):
    rows = pad_rows(advance.shape[0])
    high, low = split_array(jnp.pad(advance, ((0, rows - advance.shape[0]), (0, 0))))
    return jnp.concatenate([high, low], axis=0), high


def on_device(frames, labels, proj, phase, class_weights, velocity):
    feat_count = lax.axis_size("feat") * proj.shape[1]
    classes = class_weights.shape[1]
    feat_scale = math.sqrt(2.0 / feat_count)
    count_all = feat_count * classes
    columns = frames.shape[0]
    pair, others, blocks, groups = units_of("feat")
    me = lax.axis_index("feat")
    labels_own = jnp.concatenate(
        [lax.dynamic_slice(labels, (owner * columns,), (columns,)) for owner in (me, me ^ (1 << pair))]
    )[None, :]
    known = spread(frames, "feat", sorted(others + [pair]))
    proj_parts = split_array(proj * F32(TURN))
    phase_turns = (phase * F32(TURN))[None, :]
    weights_now = class_weights.T
    velocity_now = velocity.T
    parts = {}
    for iteration in range(ITERS):
        look = look_parts(weights_now + MOMENTUM * velocity_now)
        partial_value = {}
        after = labels_own
        order = range(len(groups))
        if iteration > 0:
            order = sorted(order, key=lambda g: -max(u.bit_count() for u in groups[g]))
        for g in order:
            if iteration == 0:
                here = [known[j] for u in groups[g] for j in blocks[u]]
                high, low, *sums = features_call(here, proj_parts, phase_turns, look, after, 512)
                parts[g] = high, low
            else:
                sums = scores_call(look, *parts[g], after, len(groups[g]), 1024)
            partial_value.update(zip(groups[g], sums))
            after = sums[0]
        mine = gather_sum(partial_value, "feat", others)
        residual = residual_call(mine, swap(mine, "feat", pair), labels_own, classes, feat_scale)
        residual = spread(residual, "feat", others)
        gradient = None
        for g in sorted(range(len(groups)), key=lambda g: max(u.bit_count() for u in groups[g])):
            gradient = gradient_call([residual[u] for u in groups[g]], *parts[g], gradient, 1024)
        gradient = sum_over(gradient[:classes] * feat_scale, "frame")
        square_sum = sum_over(jnp.sum(gradient * gradient, keepdims=True), "feat")
        grad_rms = jnp.sqrt(square_sum / count_all + EPSILON)
        velocity_now = MOMENTUM * velocity_now - STEP_RATE * gradient / grad_rms
        weights_now = weights_now + velocity_now
    return (weights_now.T, velocity_now.T)


def solution(mesh):
    return jax.shard_map(
        on_device,
        mesh=mesh,
        in_specs=(
            P(("frame", "feat"), None),
            P("frame"),
            P(None, "feat"),
            P("feat"),
            P("feat", None),
            P("feat", None),
        ),
        out_specs=(P("feat", None), P("feat", None)),
        check_vma=False,
    )
```

```python
import functools
import math

import jax
import jax.numpy as jnp
from jax import lax
from jax.experimental import pallas as pl
from jax.experimental.pallas import tpu as pltpu
from jax.sharding import PartitionSpec as P

ITERS = 2


MOMENTUM = 0.9
STEP_RATE = 0.05
EPSILON = 1e-06

BF16 = jnp.bfloat16
F32 = jnp.float32
NN = (((1,), (0,)), ((), ()))
NT = (((1,), (1,)), ((), ()))
MAGIC = 12582912.0
TURN = 1.0 / (2.0 * math.pi)
COS = (
    0.9999992107823203,
    -19.73898035576386,
    64.92865742102978,
    -85.2716215342655,
    58.790492119989025,
    -21.071105627426505,
)
VMEM_FEATURES = 12 * 2**20
VMEM_PRODUCTS = 8 * 2**20
VMEM_RESIDUAL = 4 * 2**20
VMEM_STEP = 8 * 2**20


def split(value):
    high = value.astype(BF16)
    return high, (value - high.astype(F32)).astype(BF16)


def split_array(value):
    high = lax.reduce_precision(value, exponent_bits=8, mantissa_bits=7)
    return high.astype(BF16), (value - high).astype(BF16)


def dot(left, right, dims):
    return lax.dot_general(left, right, dims, preferred_element_type=F32)


def cos_turns(turns):
    rest = turns - ((turns + MAGIC) - MAGIC)
    square = rest * rest
    total = jnp.float32(COS[-1])
    for factor in COS[-2::-1]:
        total = total * square + jnp.float32(factor)
    return total


def pad_rows(count):
    return -(-count // 8) * 8


def tree_edges(bits):
    loads, free, arrival, edges = [0] * bits, [0] * bits, {0: 0}, []
    for level in range(1, bits + 1):
        nodes = [n for n in range(1 << bits) if n.bit_count() == level]
        for node in sorted(nodes, key=lambda n: -n):
            choices = [b for b in range(bits) if node >> b & 1]
            if len(choices) > 1 and choices[-1] == bits - 1:
                choices = choices[:-1]
            bit = min(choices, key=lambda b: loads[b])
            loads[bit] += 1
            edges.append((bit, node ^ (1 << bit), node))
    ordered = []
    while edges:
        ready = [e for e in edges if e[1] in arrival]
        cost = lambda e: max(arrival[e[1]], free[e[0]]) + 1 + (e[0] == bits - 1)
        edge = min(ready, key=lambda e: (cost(e), -sum(e[2] & c[2] == e[2] for c in edges)))
        arrival[edge[2]] = free[edge[0]] = cost(edge)
        edges.remove(edge)
        ordered.append(edge)
    return ordered, arrival


def swap(value, axis, bit):
    count = lax.axis_size(axis)
    return lax.ppermute(value, axis, [(i, i ^ (1 << bit)) for i in range(count)])


def spread(item, axis, bits):
    known = {0: item}
    for bit, parent, child in tree_edges(len(bits))[0]:
        known[child] = swap(known[parent], axis, bits[bit])
    return known


def gather_sum(items, axis, bits):
    total = dict(items)
    for bit, parent, child in reversed(tree_edges(len(bits))[0]):
        total[parent] = total[parent] + swap(total[child], axis, bits[bit])
    return total[0]


def units_of(axis):
    bits = lax.axis_size(axis).bit_length() - 1
    arrival = tree_edges(bits)[1]
    blocks = [(u, u | 1 << bits - 1) for u in range(1 << bits - 1)]
    order = sorted(range(1, len(blocks)), key=lambda u: (max(arrival[j] for j in blocks[u]), -u))
    groups = [[(u, None) for u in order[i : i + 2]] for i in range(0, len(order), 2)]
    groups[0].append((0, 1))
    return blocks, [[(0, 0)]] + groups


def blocks_in(blocks, group):
    return [j for unit, half in group for j in (blocks[unit] if half is None else blocks[unit][half : half + 1])]


def widths_of(group, columns):
    return [2 * columns if half is None else columns for _, half in group]


def hand_out(total, refs):
    left = 0
    for ref in refs:
        ref[...] = total[:, left : left + ref.shape[1]]
        left += ref.shape[1]


def features_kernel(*refs, arrays, after, width):
    frames, refs = refs[:arrays], refs[arrays:]
    p_high, p_low, phase, look, look_high = refs[:5]
    high, low, *scores, x_parts = refs[5 + after :]
    rows = look_high.shape[0]
    top = 0
    for array in frames:
        part = slice(top, top + array.shape[0])
        x_parts[0, part], x_parts[1, part] = split(array[...])
        top = part.stop
    total = None
    for start in range(0, high.shape[1], width):
        part = slice(start, start + width)
        turns = (
            dot(x_parts[0], p_high[:, part], NN)
            + dot(x_parts[0], p_low[:, part], NN)
            + dot(x_parts[1], p_high[:, part], NN)
        )
        f_high, f_low = split(cos_turns(turns + phase[:, part]))
        high[:, part] = f_high
        low[:, part] = f_low
        both = dot(look[:, part], f_high, NT)
        value = both[:rows] + both[rows:] + dot(look_high[:, part], f_low, NT)
        total = value if total is None else total + value
    hand_out(total, scores)


def features_call(frames, proj, phase, look, after, widths, width):
    count, depth = sum(widths), frames[0].shape[1]
    feats = proj[0].shape[1]
    rows = look[1].shape[0]
    whole = pl.BlockSpec(memory_space=pltpu.VMEM)
    return pl.pallas_call(
        functools.partial(features_kernel, arrays=len(frames), after=len(after), width=width),
        in_specs=[whole] * (len(frames) + 5) + [pl.BlockSpec(memory_space=pl.ANY)] * len(after),
        out_specs=[whole] * (2 + len(widths)),
        out_shape=[jax.ShapeDtypeStruct((count, feats), BF16)] * 2
        + [jax.ShapeDtypeStruct((rows, columns), F32) for columns in widths],
        scratch_shapes=[pltpu.VMEM((2, count, depth), BF16)],
        compiler_params=pltpu.CompilerParams(vmem_limit_bytes=VMEM_FEATURES),
        cost_estimate=pl.CostEstimate(
            flops=6 * count * feats * (depth + rows), bytes_accessed=4 * count * feats, transcendentals=0
        ),
        name="features",
    )(*frames, *proj, phase, *look, *after)


def scores_kernel(look, look_high, high, low, _, *scores):
    rows = look_high.shape[0]
    both = dot(look[...], high[...], NT)
    hand_out(both[:rows] + both[rows:] + dot(look_high[...], low[...], NT), scores)


def scores_call(look, high, low, after, widths):
    count, feats = high.shape
    rows = look[1].shape[0]
    whole = pl.BlockSpec(memory_space=pltpu.VMEM)
    return pl.pallas_call(
        scores_kernel,
        in_specs=[whole] * 4 + [pl.BlockSpec(memory_space=pl.ANY)],
        out_specs=[whole] * len(widths),
        out_shape=[jax.ShapeDtypeStruct((rows, columns), F32) for columns in widths],
        compiler_params=pltpu.CompilerParams(vmem_limit_bytes=VMEM_PRODUCTS),
        cost_estimate=pl.CostEstimate(
            flops=6 * count * feats * rows, bytes_accessed=4 * count * feats, transcendentals=0
        ),
        name="scores",
    )(*look, high, low, after)


def gradient_kernel(*refs, halves, first, step):
    units = len(halves)
    residual, refs = refs[:units], refs[units:]
    if first:
        high, low, gradient, parts = refs
    else:
        high, low, before, gradient, parts = refs
    rows = gradient.shape[0]
    left = 0
    for ref, half in zip(residual, halves):
        value = ref[...]
        if half is not None:
            columns = value.shape[1] // 2
            value = value[:, half * columns : (half + 1) * columns]
        parts[:, left : left + value.shape[1]] = jnp.concatenate(split(value), axis=0)
        left += value.shape[1]
    for start in range(0, gradient.shape[1], step):
        part = slice(start, start + step)
        both = dot(parts[...], high[:, part], NN)
        value = both[:rows] + both[rows:] + dot(parts[:rows], low[:, part], NN)
        gradient[:, part] = value if first else before[:, part] + value


def gradient_call(residual, halves, high, low, before, step):
    units = len(residual)
    rows = residual[0].shape[0]
    count, feats = high.shape
    first = before is None
    whole = pl.BlockSpec(memory_space=pltpu.VMEM)
    return pl.pallas_call(
        functools.partial(gradient_kernel, halves=halves, first=first, step=step),
        in_specs=[whole] * (units + 2 + (not first)),
        out_specs=whole,
        out_shape=jax.ShapeDtypeStruct((rows, feats), F32),
        input_output_aliases={} if first else {units + 2: 0},
        scratch_shapes=[pltpu.VMEM((2 * rows, count), BF16)],
        compiler_params=pltpu.CompilerParams(vmem_limit_bytes=VMEM_PRODUCTS),
        cost_estimate=pl.CostEstimate(
            flops=6 * count * feats * rows, bytes_accessed=4 * count * feats, transcendentals=0
        ),
        name="gradient",
    )(*residual, high, low, *([] if first else [before]))


def residual_kernel(mine, theirs, labels, residual, *, classes, scale):
    half = mine.shape[1] // 2
    row = lax.broadcasted_iota(jnp.int32, mine.shape, 0)
    turned = jnp.concatenate([theirs[:, half:], theirs[:, :half]], axis=1)
    value = jnp.where(row < classes, (mine[...] + turned) * F32(scale), -jnp.inf)
    exponent = jnp.exp(value - jnp.max(value, axis=0, keepdims=True))
    probability = exponent / jnp.sum(exponent, axis=0, keepdims=True)
    residual[...] = probability - (row == labels[...]).astype(F32)


def residual_call(mine, theirs, labels, classes, scale):
    return pl.pallas_call(
        functools.partial(residual_kernel, classes=classes, scale=scale),
        out_shape=jax.ShapeDtypeStruct(mine.shape, F32),
        compiler_params=pltpu.CompilerParams(vmem_limit_bytes=VMEM_RESIDUAL),
        name="residual",
    )(mine, theirs, labels)


def total_kernel(mine, theirs, gradient, tiles, *, scale):
    value = (mine[...] + theirs[...]) * F32(scale)
    gradient[...] = value
    tiles[...] = jnp.broadcast_to(jnp.sum(value * value), tiles.shape)


def total_call(mine, theirs, devices, scale):
    whole = pl.BlockSpec(memory_space=pltpu.VMEM)
    return pl.pallas_call(
        functools.partial(total_kernel, scale=scale),
        in_specs=[whole] * 2,
        out_specs=[whole] * 2,
        out_shape=[jax.ShapeDtypeStruct(mine.shape, F32), jax.ShapeDtypeStruct((devices, 8, 128), F32)],
        compiler_params=pltpu.CompilerParams(vmem_limit_bytes=VMEM_STEP),
        name="total",
    )(mine, theirs)


def look_kernel(weights, velocity, look, look_high):
    write_look(weights[...] + F32(MOMENTUM) * velocity[...], look, look_high)


def write_look(value, look, look_high):
    classes, feats = value.shape
    rows = look_high.shape[0]
    if rows > classes:
        value = jnp.concatenate([value, jnp.zeros((rows - classes, feats), F32)], axis=0)
    high, low = split(value)
    look[...] = jnp.concatenate([high, low], axis=0)
    look_high[...] = high


def step_kernel(tiles, gradient, weights, velocity, weights_out, velocity_out, *looks, count):
    classes = weights.shape[0]
    squares = jnp.sum(tiles[...], axis=0)[:1, :1]
    rate = F32(STEP_RATE) / jnp.sqrt(squares / F32(count) + F32(EPSILON))
    velocity_now = F32(MOMENTUM) * velocity[...] - gradient[:classes] * rate
    weights_now = weights[...] + velocity_now
    velocity_out[...] = velocity_now
    weights_out[...] = weights_now
    if looks:
        write_look(weights_now + F32(MOMENTUM) * velocity_now, *looks)


def looks_of(weights):
    rows, feats = pad_rows(weights.shape[0]), weights.shape[1]
    return [jax.ShapeDtypeStruct((2 * rows, feats), BF16), jax.ShapeDtypeStruct((rows, feats), BF16)]


def look_call(weights, velocity):
    whole = pl.BlockSpec(memory_space=pltpu.VMEM)
    return pl.pallas_call(
        look_kernel,
        in_specs=[whole] * 2,
        out_specs=[whole] * 2,
        out_shape=looks_of(weights),
        compiler_params=pltpu.CompilerParams(vmem_limit_bytes=VMEM_STEP),
        name="look",
    )(weights, velocity)


def step_call(tiles, gradient, weights, velocity, count, last):
    whole = pl.BlockSpec(memory_space=pltpu.VMEM)
    out_shape = [jax.ShapeDtypeStruct(weights.shape, F32)] * 2 + ([] if last else looks_of(weights))
    return pl.pallas_call(
        functools.partial(step_kernel, count=count),
        in_specs=[whole] * 4,
        out_specs=[whole] * len(out_shape),
        out_shape=out_shape,
        compiler_params=pltpu.CompilerParams(vmem_limit_bytes=VMEM_STEP),
        name="step",
    )(tiles, gradient, weights, velocity)


def first_scores(known, proj_parts, phase_turns, look, ready, blocks, groups):
    count = lax.axis_size("feat")
    columns = known[0].shape[0]
    parts, own, others, arrived, after = [], [], [], [], [ready]
    for group in groups:
        here = [known[j] for j in blocks_in(blocks, group)]
        high, low, *sums = features_call(
            here, proj_parts, phase_turns, look, after, widths_of(group, columns), 512
        )
        parts.append((high, low))
        after = [sums[0]] + arrived
        arrived = []
        for (unit, _), value in zip(group, sums):
            if unit == 0:
                own.append(value)
            else:
                arrived.append(lax.ppermute(value, "feat", [(i, i ^ unit) for i in range(count)]))
        others += arrived
    return parts, sum(others, jnp.concatenate(own, axis=1))


def next_scores(parts, look, groups, columns):
    after, own, found = look[1], [], {}
    for group, (high, low) in zip(reversed(groups), reversed(parts)):
        sums = scores_call(look, high, low, after, widths_of(group, columns))
        after = sums[0]
        for (unit, half), value in zip(group, sums):
            found[unit, half] = value
    found[0, None] = jnp.concatenate([found.pop((0, 0)), found.pop((0, 1))], axis=1)
    bits = lax.axis_size("feat").bit_length() - 2
    return gather_sum({unit: value for (unit, _), value in found.items()}, "feat", list(range(bits)))


def on_device(frames, labels, proj, phase, class_weights, velocity):
    feat_count = lax.axis_size("feat") * proj.shape[1]
    classes = class_weights.shape[1]
    feat_scale = math.sqrt(2.0 / feat_count)
    count_all = feat_count * classes
    columns = frames.shape[0]
    bits = lax.axis_size("feat").bit_length() - 1
    blocks, groups = units_of("feat")
    me = lax.axis_index("feat")
    labels_own = jnp.concatenate(
        [lax.dynamic_slice(labels, (owner * columns,), (columns,)) for owner in (me, me ^ (1 << bits - 1))]
    )[None, :]
    known = spread(frames, "feat", list(range(bits)))
    proj_parts = split_array(proj * F32(TURN))
    phase_turns = (phase * F32(TURN))[None, :]
    weights_now = class_weights.T
    velocity_now = velocity.T
    look = look_call(weights_now, velocity_now)
    for iteration in range(ITERS):
        if iteration == 0:
            parts, mine = first_scores(known, proj_parts, phase_turns, look, labels_own, blocks, groups)
        else:
            mine = next_scores(parts, look, groups, columns)
        residual = residual_call(mine, swap(mine, "feat", bits - 1), labels_own, classes, feat_scale)
        residual = spread(residual, "feat", list(range(bits - 1)))
        gradient = None
        for group, (high, low) in zip(groups, parts):
            gradient = gradient_call(
                [residual[u] for u, _ in group], [half for _, half in group], high, low, gradient, 1024
            )
        gradient, tiles = total_call(gradient, swap(gradient, "frame", 0), 1 << bits, feat_scale)
        tiles = lax.all_to_all(tiles, "feat", 0, 0)
        weights_now, velocity_now, *look = step_call(
            tiles, gradient, weights_now, velocity_now, count_all, iteration == ITERS - 1
        )
    return (weights_now.T, velocity_now.T)


def solution(mesh):
    return jax.shard_map(
        on_device,
        mesh=mesh,
        in_specs=(
            P(("frame", "feat"), None),
            P("frame"),
            P(None, "feat"),
            P("feat"),
            P("feat", None),
            P("feat", None),
        ),
        out_specs=(P("feat", None), P("feat", None)),
        check_vma=False,
    )
```

```python
import functools
import math

import jax
import jax.numpy as jnp
from jax import lax
from jax.experimental import pallas as pl
from jax.experimental.pallas import tpu as pltpu
from jax.sharding import PartitionSpec as P

ITERS = 2


MOMENTUM = 0.9
STEP_RATE = 0.05
EPSILON = 1e-06

BF16 = jnp.bfloat16
F32 = jnp.float32
NN = (((1,), (0,)), ((), ()))
NT = (((1,), (1,)), ((), ()))
MAGIC = 12582912.0
TURN = 1.0 / (2.0 * math.pi)
COS = (
    0.9999992107823203,
    -19.73898035576386,
    64.92865742102978,
    -85.2716215342655,
    58.790492119989025,
    -21.071105627426505,
)
VMEM_FEATURES = 12 * 2**20
VMEM_PRODUCTS = 8 * 2**20
VMEM_RESIDUAL = 4 * 2**20
VMEM_STEP = 8 * 2**20


def split(value):
    high = value.astype(BF16)
    return high, (value - high.astype(F32)).astype(BF16)


def split_array(value):
    high = lax.reduce_precision(value, exponent_bits=8, mantissa_bits=7)
    return high.astype(BF16), (value - high).astype(BF16)


def dot(left, right, dims):
    return lax.dot_general(left, right, dims, preferred_element_type=F32)


def cos_turns(turns):
    rest = turns - ((turns + MAGIC) - MAGIC)
    square = rest * rest
    total = jnp.float32(COS[-1])
    for factor in COS[-2::-1]:
        total = total * square + jnp.float32(factor)
    return total


def pad_rows(count):
    return -(-count // 8) * 8


def tree_edges(bits):
    loads, free, arrival, edges = [0] * bits, [0] * bits, {0: 0}, []
    for level in range(1, bits + 1):
        nodes = [n for n in range(1 << bits) if n.bit_count() == level]
        for node in sorted(nodes, key=lambda n: -n):
            choices = [b for b in range(bits) if node >> b & 1]
            if len(choices) > 1 and choices[-1] == bits - 1:
                choices = choices[:-1]
            bit = min(choices, key=lambda b: loads[b])
            loads[bit] += 1
            edges.append((bit, node ^ (1 << bit), node))
    ordered = []
    while edges:
        ready = [e for e in edges if e[1] in arrival]
        cost = lambda e: max(arrival[e[1]], free[e[0]]) + 1 + (e[0] == bits - 1)
        edge = min(ready, key=lambda e: (cost(e), -sum(e[2] & c[2] == e[2] for c in edges)))
        arrival[edge[2]] = free[edge[0]] = cost(edge)
        edges.remove(edge)
        ordered.append(edge)
    return ordered, arrival


def swap(value, axis, bit):
    count = lax.axis_size(axis)
    return lax.ppermute(value, axis, [(i, i ^ (1 << bit)) for i in range(count)])


def spread(item, axis, bits):
    known = {0: item}
    for bit, parent, child in tree_edges(len(bits))[0]:
        known[child] = swap(known[parent], axis, bits[bit])
    return known


def gather_sum(items, axis, bits):
    total = dict(items)
    for bit, parent, child in reversed(tree_edges(len(bits))[0]):
        total[parent] = total[parent] + swap(total[child], axis, bits[bit])
    return total[0]


def units_of(axis):
    bits = lax.axis_size(axis).bit_length() - 1
    arrival = tree_edges(bits)[1]
    blocks = [(u, u | 1 << bits - 1) for u in range(1 << bits - 1)]
    order = sorted(range(1, len(blocks)), key=lambda u: (max(arrival[j] for j in blocks[u]), -u))
    groups = [[(u, None) for u in order[i : i + 2]] for i in range(0, len(order), 2)]
    groups[0].append((0, 1))
    return blocks, [[(0, 0)]] + groups


def blocks_in(blocks, group):
    return [j for unit, half in group for j in (blocks[unit] if half is None else blocks[unit][half : half + 1])]


def widths_of(group, columns):
    return [2 * columns if half is None else columns for _, half in group]


def hand_out(total, refs):
    left = 0
    for ref in refs:
        ref[...] = total[:, left : left + ref.shape[1]]
        left += ref.shape[1]


def features_kernel(*refs, arrays, after, width):
    frames, refs = refs[:arrays], refs[arrays:]
    p_high, p_low, phase, look, look_high = refs[:5]
    high, low, *scores, x_parts, total = refs[5 + after :]
    rows = look_high.shape[0]
    top = 0
    for array in frames:
        part = slice(top, top + array.shape[0])
        x_parts[0, part], x_parts[1, part] = split(array[...])
        top = part.stop

    total[...] = jnp.zeros(total.shape, F32)

    def chunk(i, carry):
        part = pl.ds(pl.multiple_of(i * width, width), width)
        turns = (
            dot(x_parts[0], p_high[:, part], NN)
            + dot(x_parts[0], p_low[:, part], NN)
            + dot(x_parts[1], p_high[:, part], NN)
        )
        f_high, f_low = split(cos_turns(turns + phase[:, part]))
        high[:, part] = f_high
        low[:, part] = f_low
        both = dot(look[:, part], f_high, NT)
        total[...] += both[:rows] + both[rows:] + dot(look_high[:, part], f_low, NT)
        return carry

    lax.fori_loop(0, high.shape[1] // width, chunk, 0)
    hand_out(total, scores)


def features_call(frames, proj, phase, look, after, widths, width):
    count, depth = sum(widths), frames[0].shape[1]
    feats = proj[0].shape[1]
    rows = look[1].shape[0]
    whole = pl.BlockSpec(memory_space=pltpu.VMEM)
    return pl.pallas_call(
        functools.partial(features_kernel, arrays=len(frames), after=len(after), width=width),
        in_specs=[whole] * (len(frames) + 5) + [pl.BlockSpec(memory_space=pl.ANY)] * len(after),
        out_specs=[whole] * (2 + len(widths)),
        out_shape=[jax.ShapeDtypeStruct((count, feats), BF16)] * 2
        + [jax.ShapeDtypeStruct((rows, columns), F32) for columns in widths],
        scratch_shapes=[pltpu.VMEM((2, count, depth), BF16), pltpu.VMEM((rows, count), F32)],
        compiler_params=pltpu.CompilerParams(vmem_limit_bytes=VMEM_FEATURES),
        cost_estimate=pl.CostEstimate(
            flops=6 * count * feats * (depth + rows), bytes_accessed=4 * count * feats, transcendentals=0
        ),
        name="features",
    )(*frames, *proj, phase, *look, *after)


def scores_kernel(look, look_high, high, low, _, *scores):
    rows = look_high.shape[0]
    both = dot(look[...], high[...], NT)
    hand_out(both[:rows] + both[rows:] + dot(look_high[...], low[...], NT), scores)


def scores_call(look, high, low, after, widths):
    count, feats = high.shape
    rows = look[1].shape[0]
    whole = pl.BlockSpec(memory_space=pltpu.VMEM)
    return pl.pallas_call(
        scores_kernel,
        in_specs=[whole] * 4 + [pl.BlockSpec(memory_space=pl.ANY)],
        out_specs=[whole] * len(widths),
        out_shape=[jax.ShapeDtypeStruct((rows, columns), F32) for columns in widths],
        compiler_params=pltpu.CompilerParams(vmem_limit_bytes=VMEM_PRODUCTS),
        cost_estimate=pl.CostEstimate(
            flops=6 * count * feats * rows, bytes_accessed=4 * count * feats, transcendentals=0
        ),
        name="scores",
    )(*look, high, low, after)


def gradient_kernel(*refs, halves, first, step):
    units = len(halves)
    residual, refs = refs[:units], refs[units:]
    if first:
        high, low, gradient, parts = refs
    else:
        high, low, before, gradient, parts = refs
    rows = gradient.shape[0]
    left = 0
    for ref, half in zip(residual, halves):
        value = ref[...]
        if half is not None:
            columns = value.shape[1] // 2
            value = value[:, half * columns : (half + 1) * columns]
        parts[:, left : left + value.shape[1]] = jnp.concatenate(split(value), axis=0)
        left += value.shape[1]

    def chunk(i, _):
        part = pl.ds(pl.multiple_of(i * step, step), step)
        both = dot(parts[...], high[:, part], NN)
        value = both[:rows] + both[rows:] + dot(parts[:rows], low[:, part], NN)
        gradient[:, part] = value if first else before[:, part] + value
        return _

    lax.fori_loop(0, gradient.shape[1] // step, chunk, 0)


def gradient_call(residual, halves, high, low, before, step):
    units = len(residual)
    rows = residual[0].shape[0]
    count, feats = high.shape
    first = before is None
    whole = pl.BlockSpec(memory_space=pltpu.VMEM)
    return pl.pallas_call(
        functools.partial(gradient_kernel, halves=halves, first=first, step=step),
        in_specs=[whole] * (units + 2 + (not first)),
        out_specs=whole,
        out_shape=jax.ShapeDtypeStruct((rows, feats), F32),
        input_output_aliases={} if first else {units + 2: 0},
        scratch_shapes=[pltpu.VMEM((2 * rows, count), BF16)],
        compiler_params=pltpu.CompilerParams(vmem_limit_bytes=VMEM_PRODUCTS),
        cost_estimate=pl.CostEstimate(
            flops=6 * count * feats * rows, bytes_accessed=4 * count * feats, transcendentals=0
        ),
        name="gradient",
    )(*residual, high, low, *([] if first else [before]))


def residual_kernel(mine, theirs, labels, residual, *, classes, scale):
    half = mine.shape[1] // 2
    row = lax.broadcasted_iota(jnp.int32, mine.shape, 0)
    turned = jnp.concatenate([theirs[:, half:], theirs[:, :half]], axis=1)
    value = jnp.where(row < classes, (mine[...] + turned) * F32(scale), -jnp.inf)
    exponent = jnp.exp(value - jnp.max(value, axis=0, keepdims=True))
    probability = exponent / jnp.sum(exponent, axis=0, keepdims=True)
    residual[...] = probability - (row == labels[...]).astype(F32)


def residual_call(mine, theirs, labels, classes, scale):
    return pl.pallas_call(
        functools.partial(residual_kernel, classes=classes, scale=scale),
        out_shape=jax.ShapeDtypeStruct(mine.shape, F32),
        compiler_params=pltpu.CompilerParams(vmem_limit_bytes=VMEM_RESIDUAL),
        name="residual",
    )(mine, theirs, labels)


def total_kernel(mine, theirs, gradient, tiles, *, scale):
    value = (mine[...] + theirs[...]) * F32(scale)
    gradient[...] = value
    tiles[...] = jnp.broadcast_to(jnp.sum(value * value), tiles.shape)


def total_call(mine, theirs, devices, scale):
    whole = pl.BlockSpec(memory_space=pltpu.VMEM)
    return pl.pallas_call(
        functools.partial(total_kernel, scale=scale),
        in_specs=[whole] * 2,
        out_specs=[whole] * 2,
        out_shape=[jax.ShapeDtypeStruct(mine.shape, F32), jax.ShapeDtypeStruct((devices, 8, 128), F32)],
        compiler_params=pltpu.CompilerParams(vmem_limit_bytes=VMEM_STEP),
        name="total",
    )(mine, theirs)


def look_kernel(weights, velocity, look, look_high):
    write_look(weights[...] + F32(MOMENTUM) * velocity[...], look, look_high)


def write_look(value, look, look_high):
    classes, feats = value.shape
    rows = look_high.shape[0]
    if rows > classes:
        value = jnp.concatenate([value, jnp.zeros((rows - classes, feats), F32)], axis=0)
    high, low = split(value)
    look[...] = jnp.concatenate([high, low], axis=0)
    look_high[...] = high


def step_kernel(tiles, gradient, weights, velocity, weights_out, velocity_out, *looks, count):
    classes = weights.shape[0]
    squares = jnp.sum(tiles[...], axis=0)[:1, :1]
    rate = F32(STEP_RATE) / jnp.sqrt(squares / F32(count) + F32(EPSILON))
    velocity_now = F32(MOMENTUM) * velocity[...] - gradient[:classes] * rate
    weights_now = weights[...] + velocity_now
    velocity_out[...] = velocity_now
    weights_out[...] = weights_now
    if looks:
        write_look(weights_now + F32(MOMENTUM) * velocity_now, *looks)


def looks_of(weights):
    rows, feats = pad_rows(weights.shape[0]), weights.shape[1]
    return [jax.ShapeDtypeStruct((2 * rows, feats), BF16), jax.ShapeDtypeStruct((rows, feats), BF16)]


def look_call(weights, velocity):
    whole = pl.BlockSpec(memory_space=pltpu.VMEM)
    return pl.pallas_call(
        look_kernel,
        in_specs=[whole] * 2,
        out_specs=[whole] * 2,
        out_shape=looks_of(weights),
        compiler_params=pltpu.CompilerParams(vmem_limit_bytes=VMEM_STEP),
        name="look",
    )(weights, velocity)


def step_call(tiles, gradient, weights, velocity, count, last):
    whole = pl.BlockSpec(memory_space=pltpu.VMEM)
    out_shape = [jax.ShapeDtypeStruct(weights.shape, F32)] * 2 + ([] if last else looks_of(weights))
    return pl.pallas_call(
        functools.partial(step_kernel, count=count),
        in_specs=[whole] * 4,
        out_specs=[whole] * len(out_shape),
        out_shape=out_shape,
        compiler_params=pltpu.CompilerParams(vmem_limit_bytes=VMEM_STEP),
        name="step",
    )(tiles, gradient, weights, velocity)


def first_scores(known, proj_parts, phase_turns, look, ready, blocks, groups):
    count = lax.axis_size("feat")
    columns = known[0].shape[0]
    parts, own, others, arrived, after = [], [], [], [], [ready]
    for group in groups:
        here = [known[j] for j in blocks_in(blocks, group)]
        high, low, *sums = features_call(
            here, proj_parts, phase_turns, look, after, widths_of(group, columns), 512
        )
        parts.append((high, low))
        after = [sums[0]] + arrived
        arrived = []
        for (unit, _), value in zip(group, sums):
            if unit == 0:
                own.append(value)
            else:
                arrived.append(lax.ppermute(value, "feat", [(i, i ^ unit) for i in range(count)]))
        others += arrived
    return parts, sum(others, jnp.concatenate(own, axis=1))


def next_scores(parts, look, groups, columns):
    after, own, found = look[1], [], {}
    for group, (high, low) in zip(reversed(groups), reversed(parts)):
        sums = scores_call(look, high, low, after, widths_of(group, columns))
        after = sums[0]
        for (unit, half), value in zip(group, sums):
            found[unit, half] = value
    found[0, None] = jnp.concatenate([found.pop((0, 0)), found.pop((0, 1))], axis=1)
    bits = lax.axis_size("feat").bit_length() - 2
    return gather_sum({unit: value for (unit, _), value in found.items()}, "feat", list(range(bits)))


def on_device(frames, labels, proj, phase, class_weights, velocity):
    feat_count = lax.axis_size("feat") * proj.shape[1]
    classes = class_weights.shape[1]
    feat_scale = math.sqrt(2.0 / feat_count)
    count_all = feat_count * classes
    columns = frames.shape[0]
    bits = lax.axis_size("feat").bit_length() - 1
    blocks, groups = units_of("feat")
    me = lax.axis_index("feat")
    labels_own = jnp.concatenate(
        [lax.dynamic_slice(labels, (owner * columns,), (columns,)) for owner in (me, me ^ (1 << bits - 1))]
    )[None, :]
    known = spread(frames, "feat", list(range(bits)))
    proj_parts = split_array(proj * F32(TURN))
    phase_turns = (phase * F32(TURN))[None, :]
    weights_now = class_weights.T
    velocity_now = velocity.T
    look = look_call(weights_now, velocity_now)
    for iteration in range(ITERS):
        if iteration == 0:
            parts, mine = first_scores(known, proj_parts, phase_turns, look, labels_own, blocks, groups)
        else:
            mine = next_scores(parts, look, groups, columns)
        residual = residual_call(mine, swap(mine, "feat", bits - 1), labels_own, classes, feat_scale)
        residual = spread(residual, "feat", list(range(bits - 1)))
        gradient = None
        for group, (high, low) in zip(groups, parts):
            gradient = gradient_call(
                [residual[u] for u, _ in group], [half for _, half in group], high, low, gradient, 1024
            )
        gradient, tiles = total_call(gradient, swap(gradient, "frame", 0), 1 << bits, feat_scale)
        tiles = lax.all_to_all(tiles, "feat", 0, 0)
        weights_now, velocity_now, *look = step_call(
            tiles, gradient, weights_now, velocity_now, count_all, iteration == ITERS - 1
        )
    return (weights_now.T, velocity_now.T)


def solution(mesh):
    return jax.shard_map(
        on_device,
        mesh=mesh,
        in_specs=(
            P(("frame", "feat"), None),
            P("frame"),
            P(None, "feat"),
            P("feat"),
            P("feat", None),
            P("feat", None),
        ),
        out_specs=(P("feat", None), P("feat", None)),
        check_vma=False,
    )
```

```python
import functools
import math

import jax
import jax.numpy as jnp
from jax import lax
from jax.experimental import pallas as pl
from jax.experimental.pallas import tpu as pltpu
from jax.sharding import PartitionSpec as P

ITERS = 2


MOMENTUM = 0.9
STEP_RATE = 0.05
EPSILON = 1e-06

BF16 = jnp.bfloat16
F32 = jnp.float32
NN = (((1,), (0,)), ((), ()))
NT = (((1,), (1,)), ((), ()))
MAGIC = 12582912.0
TURN = 1.0 / (2.0 * math.pi)
COS = (
    0.9999992107823203,
    -19.73898035576386,
    64.92865742102978,
    -85.2716215342655,
    58.790492119989025,
    -21.071105627426505,
)
VMEM_FEATURES = 12 * 2**20
VMEM_PRODUCTS = 8 * 2**20
VMEM_RESIDUAL = 4 * 2**20
VMEM_STEP = 8 * 2**20


def split(value):
    high = value.astype(BF16)
    return high, (value - high.astype(F32)).astype(BF16)


def split_array(value):
    high = lax.reduce_precision(value, exponent_bits=8, mantissa_bits=7)
    return high.astype(BF16), (value - high).astype(BF16)


def dot(left, right, dims):
    return lax.dot_general(left, right, dims, preferred_element_type=F32)


def cos_turns(turns):
    rest = turns - ((turns + MAGIC) - MAGIC)
    square = rest * rest
    total = jnp.float32(COS[-1])
    for factor in COS[-2::-1]:
        total = total * square + jnp.float32(factor)
    return total


def pad_rows(count):
    return -(-count // 8) * 8


def tree_edges(bits):
    loads, free, arrival, edges = [0] * bits, [0] * bits, {0: 0}, []
    for level in range(1, bits + 1):
        nodes = [n for n in range(1 << bits) if n.bit_count() == level]
        for node in sorted(nodes, key=lambda n: -n):
            choices = [b for b in range(bits) if node >> b & 1]
            if len(choices) > 1 and choices[-1] == bits - 1:
                choices = choices[:-1]
            bit = min(choices, key=lambda b: loads[b])
            loads[bit] += 1
            edges.append((bit, node ^ (1 << bit), node))
    ordered = []
    while edges:
        ready = [e for e in edges if e[1] in arrival]
        cost = lambda e: max(arrival[e[1]], free[e[0]]) + 1 + (e[0] == bits - 1)
        edge = min(ready, key=lambda e: (cost(e), -sum(e[2] & c[2] == e[2] for c in edges)))
        arrival[edge[2]] = free[edge[0]] = cost(edge)
        edges.remove(edge)
        ordered.append(edge)
    return ordered, arrival


def swap(value, axis, bit):
    count = lax.axis_size(axis)
    return lax.ppermute(value, axis, [(i, i ^ (1 << bit)) for i in range(count)])


def spread(item, axis, bits):
    known = {0: item}
    for bit, parent, child in tree_edges(len(bits))[0]:
        known[child] = swap(known[parent], axis, bits[bit])
    return known


def gather_sum(items, axis, bits):
    total = dict(items)
    for bit, parent, child in reversed(tree_edges(len(bits))[0]):
        total[parent] = total[parent] + swap(total[child], axis, bits[bit])
    return total[0]


def units_of(axis):
    bits = lax.axis_size(axis).bit_length() - 1
    arrival = tree_edges(bits)[1]
    blocks = [(u, u | 1 << bits - 1) for u in range(1 << bits - 1)]
    order = sorted(range(1, len(blocks)), key=lambda u: (max(arrival[j] for j in blocks[u]), -u))
    groups = [[(u, None) for u in order[i : i + 2]] for i in range(0, len(order), 2)]
    groups[0].append((0, 1))
    return blocks, [[(0, 0)]] + groups


def blocks_in(blocks, group):
    return [j for unit, half in group for j in (blocks[unit] if half is None else blocks[unit][half : half + 1])]


def widths_of(group, columns):
    return [2 * columns if half is None else columns for _, half in group]


def hand_out(total, refs):
    left = 0
    for ref in refs:
        ref[...] = total[:, left : left + ref.shape[1]]
        left += ref.shape[1]


def features_kernel(*refs, arrays, after, width):
    frames, refs = refs[:arrays], refs[arrays:]
    p_high, p_low, phase, look, look_high = refs[:5]
    high, low, *scores, x_parts, total = refs[5 + after :]
    rows = look_high.shape[0]
    top = 0
    for array in frames:
        part = slice(top, top + array.shape[0])
        x_parts[0, part], x_parts[1, part] = split(array[...])
        top = part.stop

    total[...] = jnp.zeros(total.shape, F32)

    def chunk(i, carry):
        part = pl.ds(pl.multiple_of(i * width, width), width)
        turns = (
            dot(x_parts[0], p_high[:, part], NN)
            + dot(x_parts[0], p_low[:, part], NN)
            + dot(x_parts[1], p_high[:, part], NN)
        )
        f_high, f_low = split(cos_turns(turns + phase[:, part]))
        high[:, part] = f_high
        low[:, part] = f_low
        both = dot(look[:, part], f_high, NT)
        total[...] += both[:rows] + both[rows:] + dot(look_high[:, part], f_low, NT)
        return carry

    lax.fori_loop(0, high.shape[1] // width, chunk, 0)
    hand_out(total, scores)


def features_call(frames, proj, phase, look, after, widths, width):
    count, depth = sum(widths), frames[0].shape[1]
    feats = proj[0].shape[1]
    rows = look[1].shape[0]
    whole = pl.BlockSpec(memory_space=pltpu.VMEM)
    return pl.pallas_call(
        functools.partial(features_kernel, arrays=len(frames), after=len(after), width=width),
        in_specs=[whole] * (len(frames) + 5) + [pl.BlockSpec(memory_space=pl.ANY)] * len(after),
        out_specs=[whole] * (2 + len(widths)),
        out_shape=[jax.ShapeDtypeStruct((count, feats), BF16)] * 2
        + [jax.ShapeDtypeStruct((rows, columns), F32) for columns in widths],
        scratch_shapes=[pltpu.VMEM((2, count, depth), BF16), pltpu.VMEM((rows, count), F32)],
        compiler_params=pltpu.CompilerParams(vmem_limit_bytes=VMEM_FEATURES),
        cost_estimate=pl.CostEstimate(
            flops=6 * count * feats * (depth + rows), bytes_accessed=4 * count * feats, transcendentals=0
        ),
        name="features",
    )(*frames, *proj, phase, *look, *after)


def scores_kernel(look, look_high, high, low, _, *scores):
    rows = look_high.shape[0]
    both = dot(look[...], high[...], NT)
    hand_out(both[:rows] + both[rows:] + dot(look_high[...], low[...], NT), scores)


def scores_call(look, high, low, after, widths):
    count, feats = high.shape
    rows = look[1].shape[0]
    whole = pl.BlockSpec(memory_space=pltpu.VMEM)
    return pl.pallas_call(
        scores_kernel,
        in_specs=[whole] * 4 + [pl.BlockSpec(memory_space=pl.ANY)],
        out_specs=[whole] * len(widths),
        out_shape=[jax.ShapeDtypeStruct((rows, columns), F32) for columns in widths],
        compiler_params=pltpu.CompilerParams(vmem_limit_bytes=VMEM_PRODUCTS),
        cost_estimate=pl.CostEstimate(
            flops=6 * count * feats * rows, bytes_accessed=4 * count * feats, transcendentals=0
        ),
        name="scores",
    )(*look, high, low, after)


def gradient_kernel(*refs, halves, first, step, start):
    units = len(halves)
    residual, refs = refs[:units], refs[units:]
    if first:
        high, low, gradient, parts = refs
    else:
        high, low, before, gradient, parts = refs
    rows = gradient.shape[0]
    left = 0
    for ref, half in zip(residual, halves):
        value = ref[...]
        if half is not None:
            columns = value.shape[1] // 2
            value = value[:, half * columns : (half + 1) * columns]
        parts[:, left : left + value.shape[1]] = jnp.concatenate(split(value), axis=0)
        left += value.shape[1]

    def chunk(i, _):
        part = pl.ds(pl.multiple_of(start + i * step, step), step)
        both = dot(parts[...], high[:, part], NN)
        value = both[:rows] + both[rows:] + dot(parts[:rows], low[:, part], NN)
        gradient[:, pl.ds(pl.multiple_of(i * step, step), step)] = value if first else before[:, part] + value
        return _

    lax.fori_loop(0, gradient.shape[1] // step, chunk, 0)


def gradient_call(residual, halves, high, low, before, step, start=0, end=None):
    units = len(residual)
    rows = residual[0].shape[0]
    count, feats = high.shape
    first = before is None
    whole = pl.BlockSpec(memory_space=pltpu.VMEM)
    return pl.pallas_call(
        functools.partial(gradient_kernel, halves=halves, first=first, step=step, start=start),
        in_specs=[whole] * (units + 2 + (not first)),
        out_specs=whole,
        out_shape=jax.ShapeDtypeStruct((rows, (end or feats) - start), F32),
        input_output_aliases={} if first or end else {units + 2: 0},
        scratch_shapes=[pltpu.VMEM((2 * rows, count), BF16)],
        compiler_params=pltpu.CompilerParams(vmem_limit_bytes=VMEM_PRODUCTS),
        cost_estimate=pl.CostEstimate(
            flops=6 * count * feats * rows, bytes_accessed=4 * count * feats, transcendentals=0
        ),
        name="gradient",
    )(*residual, high, low, *([] if first else [before]))


def residual_kernel(mine, theirs, labels, residual, *, classes, scale):
    half = mine.shape[1] // 2
    row = lax.broadcasted_iota(jnp.int32, mine.shape, 0)
    turned = jnp.concatenate([theirs[:, half:], theirs[:, :half]], axis=1)
    value = jnp.where(row < classes, (mine[...] + turned) * F32(scale), -jnp.inf)
    exponent = jnp.exp(value - jnp.max(value, axis=0, keepdims=True))
    probability = exponent / jnp.sum(exponent, axis=0, keepdims=True)
    residual[...] = probability - (row == labels[...]).astype(F32)


def residual_call(mine, theirs, labels, classes, scale):
    return pl.pallas_call(
        functools.partial(residual_kernel, classes=classes, scale=scale),
        out_shape=jax.ShapeDtypeStruct(mine.shape, F32),
        compiler_params=pltpu.CompilerParams(vmem_limit_bytes=VMEM_RESIDUAL),
        name="residual",
    )(mine, theirs, labels)


def total_kernel(*refs, scale):
    *halves, gradient, tiles = refs
    left, squares = 0, 0.0
    for mine, theirs in zip(halves[::2], halves[1::2]):
        value = (mine[...] + theirs[...]) * F32(scale)
        gradient[:, left : left + value.shape[1]] = value
        left += value.shape[1]
        squares += jnp.sum(value * value)
    tiles[...] = jnp.broadcast_to(squares, tiles.shape)


def total_call(halves, devices, scale):
    whole = pl.BlockSpec(memory_space=pltpu.VMEM)
    rows, feats = halves[0].shape[0], sum(half.shape[1] for half in halves[::2])
    return pl.pallas_call(
        functools.partial(total_kernel, scale=scale),
        in_specs=[whole] * len(halves),
        out_specs=[whole] * 2,
        out_shape=[
            jax.ShapeDtypeStruct((rows, feats), F32),
            jax.ShapeDtypeStruct((devices, 8, 128), F32),
        ],
        compiler_params=pltpu.CompilerParams(vmem_limit_bytes=VMEM_STEP),
        name="total",
    )(*halves)


def look_kernel(weights, velocity, look, look_high):
    write_look(weights[...] + F32(MOMENTUM) * velocity[...], look, look_high)


def write_look(value, look, look_high):
    classes, feats = value.shape
    rows = look_high.shape[0]
    if rows > classes:
        value = jnp.concatenate([value, jnp.zeros((rows - classes, feats), F32)], axis=0)
    high, low = split(value)
    look[...] = jnp.concatenate([high, low], axis=0)
    look_high[...] = high


def step_kernel(tiles, gradient, weights, velocity, weights_out, velocity_out, *looks, count):
    classes = weights.shape[0]
    squares = jnp.sum(tiles[...], axis=0)[:1, :1]
    rate = F32(STEP_RATE) / jnp.sqrt(squares / F32(count) + F32(EPSILON))
    velocity_now = F32(MOMENTUM) * velocity[...] - gradient[:classes] * rate
    weights_now = weights[...] + velocity_now
    velocity_out[...] = velocity_now
    weights_out[...] = weights_now
    if looks:
        write_look(weights_now + F32(MOMENTUM) * velocity_now, *looks)


def looks_of(weights):
    rows, feats = pad_rows(weights.shape[0]), weights.shape[1]
    return [jax.ShapeDtypeStruct((2 * rows, feats), BF16), jax.ShapeDtypeStruct((rows, feats), BF16)]


def look_call(weights, velocity):
    whole = pl.BlockSpec(memory_space=pltpu.VMEM)
    return pl.pallas_call(
        look_kernel,
        in_specs=[whole] * 2,
        out_specs=[whole] * 2,
        out_shape=looks_of(weights),
        compiler_params=pltpu.CompilerParams(vmem_limit_bytes=VMEM_STEP),
        name="look",
    )(weights, velocity)


def step_call(tiles, gradient, weights, velocity, count, last):
    whole = pl.BlockSpec(memory_space=pltpu.VMEM)
    out_shape = [jax.ShapeDtypeStruct(weights.shape, F32)] * 2 + ([] if last else looks_of(weights))
    return pl.pallas_call(
        functools.partial(step_kernel, count=count),
        in_specs=[whole] * 4,
        out_specs=[whole] * len(out_shape),
        out_shape=out_shape,
        compiler_params=pltpu.CompilerParams(vmem_limit_bytes=VMEM_STEP),
        name="step",
    )(tiles, gradient, weights, velocity)


def first_scores(known, proj_parts, phase_turns, look, ready, blocks, groups):
    count = lax.axis_size("feat")
    columns = known[0].shape[0]
    parts, own, others, arrived, after = [], [], [], [], [ready]
    for group in groups:
        here = [known[j] for j in blocks_in(blocks, group)]
        high, low, *sums = features_call(
            here, proj_parts, phase_turns, look, after, widths_of(group, columns), 512
        )
        parts.append((high, low))
        after = [sums[0]] + arrived
        arrived = []
        for (unit, _), value in zip(group, sums):
            if unit == 0:
                own.append(value)
            else:
                arrived.append(lax.ppermute(value, "feat", [(i, i ^ unit) for i in range(count)]))
        others += arrived
    return parts, sum(others, jnp.concatenate(own, axis=1))


def next_scores(parts, look, groups, columns):
    after, own, found = look[1], [], {}
    for group, (high, low) in zip(reversed(groups), reversed(parts)):
        sums = scores_call(look, high, low, after, widths_of(group, columns))
        after = sums[0]
        for (unit, half), value in zip(group, sums):
            found[unit, half] = value
    found[0, None] = jnp.concatenate([found.pop((0, 0)), found.pop((0, 1))], axis=1)
    bits = lax.axis_size("feat").bit_length() - 2
    return gather_sum({unit: value for (unit, _), value in found.items()}, "feat", list(range(bits)))


def on_device(frames, labels, proj, phase, class_weights, velocity):
    feat_count = lax.axis_size("feat") * proj.shape[1]
    classes = class_weights.shape[1]
    feat_scale = math.sqrt(2.0 / feat_count)
    count_all = feat_count * classes
    columns = frames.shape[0]
    bits = lax.axis_size("feat").bit_length() - 1
    blocks, groups = units_of("feat")
    me = lax.axis_index("feat")
    labels_own = jnp.concatenate(
        [lax.dynamic_slice(labels, (owner * columns,), (columns,)) for owner in (me, me ^ (1 << bits - 1))]
    )[None, :]
    known = spread(frames, "feat", list(range(bits)))
    proj_parts = split_array(proj * F32(TURN))
    phase_turns = (phase * F32(TURN))[None, :]
    weights_now = class_weights.T
    velocity_now = velocity.T
    look = look_call(weights_now, velocity_now)
    for iteration in range(ITERS):
        if iteration == 0:
            parts, mine = first_scores(known, proj_parts, phase_turns, look, labels_own, blocks, groups)
        else:
            mine = next_scores(parts, look, groups, columns)
        residual = residual_call(mine, swap(mine, "feat", bits - 1), labels_own, classes, feat_scale)
        residual = spread(residual, "feat", list(range(bits - 1)))
        gradient, halves = None, []
        for group, (high, low) in zip(groups, parts):
            here = [residual[u] for u, _ in group], [half for _, half in group], high, low
            if group is groups[-1]:
                middle = high.shape[1] // 2
                for start in (0, middle):
                    mine = gradient_call(*here, gradient, middle, start, start + middle)
                    halves += [mine, swap(mine, "frame", 0)]
            else:
                gradient = gradient_call(*here, gradient, high.shape[1] // 2)
        gradient, tiles = total_call(halves, 1 << bits, feat_scale)
        tiles = lax.all_to_all(tiles, "feat", 0, 0)
        weights_now, velocity_now, *look = step_call(
            tiles, gradient, weights_now, velocity_now, count_all, iteration == ITERS - 1
        )
    return (weights_now.T, velocity_now.T)


def solution(mesh):
    return jax.shard_map(
        on_device,
        mesh=mesh,
        in_specs=(
            P(("frame", "feat"), None),
            P("frame"),
            P(None, "feat"),
            P("feat"),
            P("feat", None),
            P("feat", None),
        ),
        out_specs=(P("feat", None), P("feat", None)),
        check_vma=False,
    )
```

```python
import functools
import math

import jax
import jax.numpy as jnp
from jax import lax
from jax.experimental import pallas as pl
from jax.experimental.pallas import tpu as pltpu
from jax.sharding import PartitionSpec as P

ITERS = 2


MOMENTUM = 0.9
STEP_RATE = 0.05
EPSILON = 1e-06

BF16 = jnp.bfloat16
F32 = jnp.float32
NN = (((1,), (0,)), ((), ()))
NT = (((1,), (1,)), ((), ()))
MAGIC = 12582912.0
TURN = 1.0 / (2.0 * math.pi)
COS = (
    0.9999992107823203,
    -19.73898035576386,
    64.92865742102978,
    -85.2716215342655,
    58.790492119989025,
    -21.071105627426505,
)
VMEM_FEATURES = 12 * 2**20
VMEM_PRODUCTS = 8 * 2**20
VMEM_RESIDUAL = 4 * 2**20
VMEM_STEP = 8 * 2**20


def split(value):
    high = value.astype(BF16)
    return high, (value - high.astype(F32)).astype(BF16)


def split_array(value):
    high = lax.reduce_precision(value, exponent_bits=8, mantissa_bits=7)
    return high.astype(BF16), (value - high).astype(BF16)


def dot(left, right, dims):
    return lax.dot_general(left, right, dims, preferred_element_type=F32)


def cos_turns(turns):
    rest = turns - ((turns + MAGIC) - MAGIC)
    square = rest * rest
    total = jnp.float32(COS[-1])
    for factor in COS[-2::-1]:
        total = total * square + jnp.float32(factor)
    return total


def pad_rows(count):
    return -(-count // 8) * 8


def tree_edges(bits):
    loads, free, arrival, edges = [0] * bits, [0] * bits, {0: 0}, []
    for level in range(1, bits + 1):
        nodes = [n for n in range(1 << bits) if n.bit_count() == level]
        for node in sorted(nodes, key=lambda n: -n):
            choices = [b for b in range(bits) if node >> b & 1]
            if len(choices) > 1 and choices[-1] == bits - 1:
                choices = choices[:-1]
            bit = min(choices, key=lambda b: loads[b])
            loads[bit] += 1
            edges.append((bit, node ^ (1 << bit), node))
    ordered = []
    while edges:
        ready = [e for e in edges if e[1] in arrival]
        cost = lambda e: max(arrival[e[1]], free[e[0]]) + 1 + (e[0] == bits - 1)
        edge = min(ready, key=lambda e: (cost(e), -sum(e[2] & c[2] == e[2] for c in edges)))
        arrival[edge[2]] = free[edge[0]] = cost(edge)
        edges.remove(edge)
        ordered.append(edge)
    return ordered, arrival


def swap(value, axis, bit):
    count = lax.axis_size(axis)
    return lax.ppermute(value, axis, [(i, i ^ (1 << bit)) for i in range(count)])


def spread(item, axis, bits):
    known = {0: item}
    for bit, parent, child in tree_edges(len(bits))[0]:
        known[child] = swap(known[parent], axis, bits[bit])
    return known


def gather_sum(items, axis, bits):
    total = dict(items)
    for bit, parent, child in reversed(tree_edges(len(bits))[0]):
        total[parent] = total[parent] + swap(total[child], axis, bits[bit])
    return total[0]


def units_of(axis):
    bits = lax.axis_size(axis).bit_length() - 1
    arrival = tree_edges(bits)[1]
    blocks = [(u, u | 1 << bits - 1) for u in range(1 << bits - 1)]
    order = sorted(range(1, len(blocks)), key=lambda u: (max(arrival[j] for j in blocks[u]), -u))
    groups = [[(u, None) for u in order[i : i + 2]] for i in range(0, len(order), 2)]
    groups[0].append((0, 1))
    return blocks, [[(0, 0)]] + groups


def blocks_in(blocks, group):
    return [j for unit, half in group for j in (blocks[unit] if half is None else blocks[unit][half : half + 1])]


def widths_of(group, columns):
    return [2 * columns if half is None else columns for _, half in group]


def hand_out(total, refs):
    left = 0
    for ref in refs:
        ref[...] = total[:, left : left + ref.shape[1]]
        left += ref.shape[1]


def features_kernel(*refs, arrays, after, width):
    frames, refs = refs[:arrays], refs[arrays:]
    p_high, p_low, phase, look, look_high = refs[:5]
    high, low, *scores, x_parts, total = refs[5 + after :]
    rows = look_high.shape[0]
    top = 0
    for array in frames:
        part = slice(top, top + array.shape[0])
        x_parts[0, part], x_parts[1, part] = split(array[...])
        top = part.stop

    total[...] = jnp.zeros(total.shape, F32)

    def chunk(i, carry):
        part = pl.ds(pl.multiple_of(i * width, width), width)
        turns = (
            dot(x_parts[0], p_high[:, part], NN)
            + dot(x_parts[0], p_low[:, part], NN)
            + dot(x_parts[1], p_high[:, part], NN)
        )
        f_high, f_low = split(cos_turns(turns + phase[:, part]))
        high[:, part] = f_high
        low[:, part] = f_low
        both = dot(look[:, part], f_high, NT)
        total[...] += both[:rows] + both[rows:] + dot(look_high[:, part], f_low, NT)
        return carry

    lax.fori_loop(0, high.shape[1] // width, chunk, 0)
    hand_out(total, scores)


def features_call(frames, proj, phase, look, after, widths, width):
    count, depth = sum(widths), frames[0].shape[1]
    feats = proj[0].shape[1]
    rows = look[1].shape[0]
    whole = pl.BlockSpec(memory_space=pltpu.VMEM)
    return pl.pallas_call(
        functools.partial(features_kernel, arrays=len(frames), after=len(after), width=width),
        in_specs=[whole] * (len(frames) + 5) + [pl.BlockSpec(memory_space=pl.ANY)] * len(after),
        out_specs=[whole] * (2 + len(widths)),
        out_shape=[jax.ShapeDtypeStruct((count, feats), BF16)] * 2
        + [jax.ShapeDtypeStruct((rows, columns), F32) for columns in widths],
        scratch_shapes=[pltpu.VMEM((2, count, depth), BF16), pltpu.VMEM((rows, count), F32)],
        compiler_params=pltpu.CompilerParams(vmem_limit_bytes=VMEM_FEATURES),
        cost_estimate=pl.CostEstimate(
            flops=8 * count * feats * (depth + rows), bytes_accessed=4 * count * feats, transcendentals=0
        ),
        name="features",
    )(*frames, *proj, phase, *look, *after)


def scores_kernel(look, look_high, high, low, _, *scores):
    rows = look_high.shape[0]
    both = dot(look[...], high[...], NT)
    hand_out(both[:rows] + both[rows:] + dot(look_high[...], low[...], NT), scores)


def scores_call(look, high, low, after, widths):
    count, feats = high.shape
    rows = look[1].shape[0]
    whole = pl.BlockSpec(memory_space=pltpu.VMEM)
    return pl.pallas_call(
        scores_kernel,
        in_specs=[whole] * 4 + [pl.BlockSpec(memory_space=pl.ANY)],
        out_specs=[whole] * len(widths),
        out_shape=[jax.ShapeDtypeStruct((rows, columns), F32) for columns in widths],
        compiler_params=pltpu.CompilerParams(vmem_limit_bytes=VMEM_PRODUCTS),
        cost_estimate=pl.CostEstimate(
            flops=8 * count * feats * rows, bytes_accessed=4 * count * feats, transcendentals=0
        ),
        name="scores",
    )(*look, high, low, after)


def gradient_kernel(*refs, halves, first, step, start):
    units = len(halves)
    residual, refs = refs[:units], refs[units:]
    if first:
        high, low, gradient, parts = refs
    else:
        high, low, before, gradient, parts = refs
    rows = gradient.shape[0]
    left = 0
    for ref, half in zip(residual, halves):
        value = ref[...]
        if half is not None:
            columns = value.shape[1] // 2
            value = value[:, half * columns : (half + 1) * columns]
        parts[:, left : left + value.shape[1]] = jnp.concatenate(split(value), axis=0)
        left += value.shape[1]

    def chunk(i, _):
        part = pl.ds(pl.multiple_of(start + i * step, step), step)
        both = dot(parts[...], high[:, part], NN)
        value = both[:rows] + both[rows:] + dot(parts[:rows], low[:, part], NN)
        gradient[:, pl.ds(pl.multiple_of(i * step, step), step)] = value if first else before[:, part] + value
        return _

    lax.fori_loop(0, gradient.shape[1] // step, chunk, 0)


def gradient_call(residual, halves, high, low, before, step, start=0, end=None):
    units = len(residual)
    rows = residual[0].shape[0]
    count, feats = high.shape
    first = before is None
    whole = pl.BlockSpec(memory_space=pltpu.VMEM)
    return pl.pallas_call(
        functools.partial(gradient_kernel, halves=halves, first=first, step=step, start=start),
        in_specs=[whole] * (units + 2 + (not first)),
        out_specs=whole,
        out_shape=jax.ShapeDtypeStruct((rows, (end or feats) - start), F32),
        input_output_aliases={} if first or end else {units + 2: 0},
        scratch_shapes=[pltpu.VMEM((2 * rows, count), BF16)],
        compiler_params=pltpu.CompilerParams(vmem_limit_bytes=VMEM_PRODUCTS),
        cost_estimate=pl.CostEstimate(
            flops=8 * count * feats * rows, bytes_accessed=4 * count * feats, transcendentals=0
        ),
        name="gradient",
    )(*residual, high, low, *([] if first else [before]))


def residual_kernel(mine, theirs, labels, residual, *, classes, scale):
    half = mine.shape[1] // 2
    row = lax.broadcasted_iota(jnp.int32, mine.shape, 0)
    turned = jnp.concatenate([theirs[:, half:], theirs[:, :half]], axis=1)
    value = jnp.where(row < classes, (mine[...] + turned) * F32(scale), -jnp.inf)
    exponent = jnp.exp(value - jnp.max(value, axis=0, keepdims=True))
    probability = exponent / jnp.sum(exponent, axis=0, keepdims=True)
    residual[...] = probability - (row == labels[...]).astype(F32)


def residual_call(mine, theirs, labels, classes, scale):
    return pl.pallas_call(
        functools.partial(residual_kernel, classes=classes, scale=scale),
        out_shape=jax.ShapeDtypeStruct(mine.shape, F32),
        compiler_params=pltpu.CompilerParams(vmem_limit_bytes=VMEM_RESIDUAL),
        name="residual",
    )(mine, theirs, labels)


def total_kernel(*refs, scale):
    *halves, gradient, tiles = refs
    left, squares = 0, 0.0
    for mine, theirs in zip(halves[::2], halves[1::2]):
        value = (mine[...] + theirs[...]) * F32(scale)
        gradient[:, left : left + value.shape[1]] = value
        left += value.shape[1]
        squares += jnp.sum(value * value)
    tiles[...] = jnp.broadcast_to(squares, tiles.shape)


def total_call(halves, devices, scale):
    whole = pl.BlockSpec(memory_space=pltpu.VMEM)
    rows, feats = halves[0].shape[0], sum(half.shape[1] for half in halves[::2])
    return pl.pallas_call(
        functools.partial(total_kernel, scale=scale),
        in_specs=[whole] * len(halves),
        out_specs=[whole] * 2,
        out_shape=[
            jax.ShapeDtypeStruct((rows, feats), F32),
            jax.ShapeDtypeStruct((devices, 8, 128), F32),
        ],
        compiler_params=pltpu.CompilerParams(vmem_limit_bytes=VMEM_STEP),
        name="total",
    )(*halves)


def look_kernel(weights, velocity, look, look_high):
    write_look(weights[...] + F32(MOMENTUM) * velocity[...], look, look_high)


def write_look(value, look, look_high):
    classes, feats = value.shape
    rows = look_high.shape[0]
    if rows > classes:
        value = jnp.concatenate([value, jnp.zeros((rows - classes, feats), F32)], axis=0)
    high, low = split(value)
    look[...] = jnp.concatenate([high, low], axis=0)
    look_high[...] = high


def step_kernel(tiles, gradient, weights, velocity, weights_out, velocity_out, *looks, count):
    classes = weights.shape[0]
    squares = jnp.sum(tiles[...], axis=0)[:1, :1]
    rate = F32(STEP_RATE) / jnp.sqrt(squares / F32(count) + F32(EPSILON))
    velocity_now = F32(MOMENTUM) * velocity[...] - gradient[:classes] * rate
    weights_now = weights[...] + velocity_now
    velocity_out[...] = velocity_now
    weights_out[...] = weights_now
    if looks:
        write_look(weights_now + F32(MOMENTUM) * velocity_now, *looks)


def looks_of(weights):
    rows, feats = pad_rows(weights.shape[0]), weights.shape[1]
    return [jax.ShapeDtypeStruct((2 * rows, feats), BF16), jax.ShapeDtypeStruct((rows, feats), BF16)]


def look_call(weights, velocity):
    whole = pl.BlockSpec(memory_space=pltpu.VMEM)
    return pl.pallas_call(
        look_kernel,
        in_specs=[whole] * 2,
        out_specs=[whole] * 2,
        out_shape=looks_of(weights),
        compiler_params=pltpu.CompilerParams(vmem_limit_bytes=VMEM_STEP),
        name="look",
    )(weights, velocity)


def step_call(tiles, gradient, weights, velocity, count, last):
    whole = pl.BlockSpec(memory_space=pltpu.VMEM)
    out_shape = [jax.ShapeDtypeStruct(weights.shape, F32)] * 2 + ([] if last else looks_of(weights))
    return pl.pallas_call(
        functools.partial(step_kernel, count=count),
        in_specs=[whole] * 4,
        out_specs=[whole] * len(out_shape),
        out_shape=out_shape,
        compiler_params=pltpu.CompilerParams(vmem_limit_bytes=VMEM_STEP),
        name="step",
    )(tiles, gradient, weights, velocity)


def first_scores(known, proj_parts, phase_turns, look, ready, blocks, groups):
    count = lax.axis_size("feat")
    columns = known[0].shape[0]
    parts, own, others, arrived, after = [], [], [], [], [ready]
    for group in groups:
        here = [known[j] for j in blocks_in(blocks, group)]
        high, low, *sums = features_call(
            here, proj_parts, phase_turns, look, after, widths_of(group, columns), 512
        )
        parts.append((high, low))
        after = [sums[0]] + arrived
        arrived = []
        for (unit, _), value in zip(group, sums):
            if unit == 0:
                own.append(value)
            else:
                arrived.append(lax.ppermute(value, "feat", [(i, i ^ unit) for i in range(count)]))
        others += arrived
    return parts, sum(others, jnp.concatenate(own, axis=1))


def next_scores(parts, look, groups, columns):
    after, own, found = look[1], [], {}
    for group, (high, low) in zip(reversed(groups), reversed(parts)):
        sums = scores_call(look, high, low, after, widths_of(group, columns))
        after = sums[0]
        for (unit, half), value in zip(group, sums):
            found[unit, half] = value
    found[0, None] = jnp.concatenate([found.pop((0, 0)), found.pop((0, 1))], axis=1)
    bits = lax.axis_size("feat").bit_length() - 2
    return gather_sum({unit: value for (unit, _), value in found.items()}, "feat", list(range(bits)))


def on_device(frames, labels, proj, phase, class_weights, velocity):
    feat_count = lax.axis_size("feat") * proj.shape[1]
    classes = class_weights.shape[1]
    feat_scale = math.sqrt(2.0 / feat_count)
    count_all = feat_count * classes
    columns = frames.shape[0]
    bits = lax.axis_size("feat").bit_length() - 1
    blocks, groups = units_of("feat")
    me = lax.axis_index("feat")
    labels_own = jnp.concatenate(
        [lax.dynamic_slice(labels, (owner * columns,), (columns,)) for owner in (me, me ^ (1 << bits - 1))]
    )[None, :]
    known = spread(frames, "feat", list(range(bits)))
    proj_parts = split_array(proj * F32(TURN))
    phase_turns = (phase * F32(TURN))[None, :]
    weights_now = class_weights.T
    velocity_now = velocity.T
    look = look_call(weights_now, velocity_now)
    for iteration in range(ITERS):
        if iteration == 0:
            parts, mine = first_scores(known, proj_parts, phase_turns, look, labels_own, blocks, groups)
        else:
            mine = next_scores(parts, look, groups, columns)
        residual = residual_call(mine, swap(mine, "feat", bits - 1), labels_own, classes, feat_scale)
        residual = spread(residual, "feat", list(range(bits - 1)))
        gradient, halves = None, []
        for group, (high, low) in zip(groups, parts):
            here = [residual[u] for u, _ in group], [half for _, half in group], high, low
            if group is groups[-1]:
                middle = high.shape[1] // 2
                for start in (0, middle):
                    mine = gradient_call(*here, gradient, middle, start, start + middle)
                    halves += [mine, swap(mine, "frame", 0)]
            else:
                gradient = gradient_call(*here, gradient, high.shape[1] // 2)
        gradient, tiles = total_call(halves, 1 << bits, feat_scale)
        tiles = lax.all_to_all(tiles, "feat", 0, 0)
        weights_now, velocity_now, *look = step_call(
            tiles, gradient, weights_now, velocity_now, count_all, iteration == ITERS - 1
        )
    return (weights_now.T, velocity_now.T)


def solution(mesh):
    return jax.shard_map(
        on_device,
        mesh=mesh,
        in_specs=(
            P(("frame", "feat"), None),
            P("frame"),
            P(None, "feat"),
            P("feat"),
            P("feat", None),
            P("feat", None),
        ),
        out_specs=(P("feat", None), P("feat", None)),
        check_vma=False,
    )
```

```python
import functools
import math

import jax
import jax.numpy as jnp
from jax import lax
from jax.experimental import pallas as pl
from jax.experimental.pallas import tpu as pltpu
from jax.sharding import PartitionSpec as P

ITERS = 2


MOMENTUM = 0.9
STEP_RATE = 0.05
EPSILON = 1e-06

BF16 = jnp.bfloat16
F32 = jnp.float32
NN = (((1,), (0,)), ((), ()))
NT = (((1,), (1,)), ((), ()))
MAGIC = 12582912.0
TURN = 1.0 / (2.0 * math.pi)
COS = (
    0.9999992107823203,
    -19.73898035576386,
    64.92865742102978,
    -85.2716215342655,
    58.790492119989025,
    -21.071105627426505,
)
VMEM_FEATURES = 12 * 2**20
VMEM_PRODUCTS = 8 * 2**20
VMEM_RESIDUAL = 4 * 2**20
VMEM_STEP = 8 * 2**20


def split(value):
    high = value.astype(BF16)
    return high, (value - high.astype(F32)).astype(BF16)


def split_array(value):
    high = lax.reduce_precision(value, exponent_bits=8, mantissa_bits=7)
    return high.astype(BF16), (value - high).astype(BF16)


def dot(left, right, dims):
    return lax.dot_general(left, right, dims, preferred_element_type=F32)


def cos_turns(turns):
    rest = turns - ((turns + MAGIC) - MAGIC)
    square = rest * rest
    total = jnp.float32(COS[-1])
    for factor in COS[-2::-1]:
        total = total * square + jnp.float32(factor)
    return total


def pad_rows(count):
    return -(-count // 8) * 8


def tree_edges(bits):
    loads, free, arrival, edges = [0] * bits, [0] * bits, {0: 0}, []
    for level in range(1, bits + 1):
        nodes = [n for n in range(1 << bits) if n.bit_count() == level]
        for node in sorted(nodes, key=lambda n: -n):
            choices = [b for b in range(bits) if node >> b & 1]
            if len(choices) > 1 and choices[-1] == bits - 1:
                choices = choices[:-1]
            bit = min(choices, key=lambda b: loads[b])
            loads[bit] += 1
            edges.append((bit, node ^ (1 << bit), node))
    ordered = []
    while edges:
        ready = [e for e in edges if e[1] in arrival]
        cost = lambda e: max(arrival[e[1]], free[e[0]]) + 1 + (e[0] == bits - 1)
        edge = min(ready, key=lambda e: (cost(e), -sum(e[2] & c[2] == e[2] for c in edges)))
        arrival[edge[2]] = free[edge[0]] = cost(edge)
        edges.remove(edge)
        ordered.append(edge)
    return ordered, arrival


def swap(value, axis, bit):
    count = lax.axis_size(axis)
    return lax.ppermute(value, axis, [(i, i ^ (1 << bit)) for i in range(count)])


def spread(item, axis, bits):
    known = {0: item}
    for bit, parent, child in tree_edges(len(bits))[0]:
        known[child] = swap(known[parent], axis, bits[bit])
    return known


def gather_sum(items, axis, bits):
    total = dict(items)
    for bit, parent, child in reversed(tree_edges(len(bits))[0]):
        total[parent] = total[parent] + swap(total[child], axis, bits[bit])
    return total[0]


def units_of(axis):
    bits = lax.axis_size(axis).bit_length() - 1
    arrival = tree_edges(bits)[1]
    blocks = [(u, u | 1 << bits - 1) for u in range(1 << bits - 1)]
    order = sorted(range(1, len(blocks)), key=lambda u: (max(arrival[j] for j in blocks[u]), -u))
    groups = [[(u, None) for u in order[i : i + 2]] for i in range(0, len(order), 2)]
    groups[0].append((0, 1))
    return blocks, [[(0, 0)]] + groups


def blocks_in(blocks, group):
    return [j for unit, half in group for j in (blocks[unit] if half is None else blocks[unit][half : half + 1])]


def widths_of(group, columns):
    return [2 * columns if half is None else columns for _, half in group]


def hand_out(total, refs):
    left = 0
    for ref in refs:
        ref[...] = total[:, left : left + ref.shape[1]]
        left += ref.shape[1]


def features_kernel(*refs, arrays, after, width):
    frames, refs = refs[:arrays], refs[arrays:]
    p_high, p_low, phase, look, look_high = refs[:5]
    high, low, *scores, x_parts, total = refs[5 + after :]
    rows = look_high.shape[0]
    top = 0
    for array in frames:
        part = slice(top, top + array.shape[0])
        x_parts[0, part], x_parts[1, part] = split(array[...])
        top = part.stop

    total[...] = jnp.zeros(total.shape, F32)

    def chunk(i, carry):
        part = pl.ds(pl.multiple_of(i * width, width), width)
        turns = (
            dot(x_parts[0], p_high[:, part], NN)
            + dot(x_parts[0], p_low[:, part], NN)
            + dot(x_parts[1], p_high[:, part], NN)
        )
        f_high, f_low = split(cos_turns(turns + phase[:, part]))
        high[:, part] = f_high
        low[:, part] = f_low
        both = dot(look[:, part], f_high, NT)
        total[...] += both[:rows] + both[rows:] + dot(look_high[:, part], f_low, NT)
        return carry

    lax.fori_loop(0, high.shape[1] // width, chunk, 0)
    hand_out(total, scores)


def features_call(frames, proj, phase, look, after, widths, width):
    count, depth = sum(widths), frames[0].shape[1]
    feats = proj[0].shape[1]
    rows = look[1].shape[0]
    whole = pl.BlockSpec(memory_space=pltpu.VMEM)
    return pl.pallas_call(
        functools.partial(features_kernel, arrays=len(frames), after=len(after), width=width),
        in_specs=[whole] * (len(frames) + 5) + [pl.BlockSpec(memory_space=pl.ANY)] * len(after),
        out_specs=[whole] * (2 + len(widths)),
        out_shape=[jax.ShapeDtypeStruct((count, feats), BF16)] * 2
        + [jax.ShapeDtypeStruct((rows, columns), F32) for columns in widths],
        scratch_shapes=[pltpu.VMEM((2, count, depth), BF16), pltpu.VMEM((rows, count), F32)],
        compiler_params=pltpu.CompilerParams(vmem_limit_bytes=VMEM_FEATURES),
        cost_estimate=pl.CostEstimate(
            flops=8 * count * feats * (depth + rows), bytes_accessed=4 * count * feats, transcendentals=0
        ),
        name="features",
    )(*frames, *proj, phase, *look, *after)


def scores_kernel(look, look_high, high, low, _, *scores):
    rows = look_high.shape[0]
    both = dot(look[...], high[...], NT)
    hand_out(both[:rows] + both[rows:] + dot(look_high[...], low[...], NT), scores)


def scores_call(look, high, low, after, widths):
    count, feats = high.shape
    rows = look[1].shape[0]
    whole = pl.BlockSpec(memory_space=pltpu.VMEM)
    return pl.pallas_call(
        scores_kernel,
        in_specs=[whole] * 4 + [pl.BlockSpec(memory_space=pl.ANY)],
        out_specs=[whole] * len(widths),
        out_shape=[jax.ShapeDtypeStruct((rows, columns), F32) for columns in widths],
        compiler_params=pltpu.CompilerParams(vmem_limit_bytes=VMEM_PRODUCTS),
        cost_estimate=pl.CostEstimate(
            flops=8 * count * feats * rows, bytes_accessed=4 * count * feats, transcendentals=0
        ),
        name="scores",
    )(*look, high, low, after)


def gradient_kernel(*refs, halves, first, step, start):
    units = len(halves)
    residual, refs = refs[:units], refs[units:]
    if first:
        high, low, gradient, parts = refs
    else:
        high, low, before, gradient, parts = refs
    rows = gradient.shape[0]
    left = 0
    for ref, half in zip(residual, halves):
        value = ref[...]
        if half is not None:
            columns = value.shape[1] // 2
            value = value[:, half * columns : (half + 1) * columns]
        parts[:, left : left + value.shape[1]] = jnp.concatenate(split(value), axis=0)
        left += value.shape[1]

    def chunk(i, _):
        part = pl.ds(pl.multiple_of(start + i * step, step), step)
        both = dot(parts[...], high[:, part], NN)
        value = both[:rows] + both[rows:] + dot(parts[:rows], low[:, part], NN)
        gradient[:, pl.ds(pl.multiple_of(i * step, step), step)] = value if first else before[:, part] + value
        return _

    lax.fori_loop(0, gradient.shape[1] // step, chunk, 0)


def gradient_call(residual, halves, high, low, before, step, start=0, end=None):
    units = len(residual)
    rows = residual[0].shape[0]
    count, feats = high.shape
    first = before is None
    whole = pl.BlockSpec(memory_space=pltpu.VMEM)
    return pl.pallas_call(
        functools.partial(gradient_kernel, halves=halves, first=first, step=step, start=start),
        in_specs=[whole] * (units + 2 + (not first)),
        out_specs=whole,
        out_shape=jax.ShapeDtypeStruct((rows, (end or feats) - start), F32),
        input_output_aliases={} if first or end else {units + 2: 0},
        scratch_shapes=[pltpu.VMEM((2 * rows, count), BF16)],
        compiler_params=pltpu.CompilerParams(vmem_limit_bytes=VMEM_PRODUCTS),
        cost_estimate=pl.CostEstimate(
            flops=8 * count * feats * rows, bytes_accessed=4 * count * feats, transcendentals=0
        ),
        name="gradient",
    )(*residual, high, low, *([] if first else [before]))


def residual_kernel(mine, theirs, labels, residual, *, classes, scale):
    half = mine.shape[1] // 2
    row = lax.broadcasted_iota(jnp.int32, mine.shape, 0)
    turned = jnp.concatenate([theirs[:, half:], theirs[:, :half]], axis=1)
    value = jnp.where(row < classes, (mine[...] + turned) * F32(scale), -jnp.inf)
    exponent = jnp.exp(value - jnp.max(value, axis=0, keepdims=True))
    probability = exponent / jnp.sum(exponent, axis=0, keepdims=True)
    residual[...] = probability - (row == labels[...]).astype(F32)


def residual_call(mine, theirs, labels, classes, scale):
    return pl.pallas_call(
        functools.partial(residual_kernel, classes=classes, scale=scale),
        out_shape=jax.ShapeDtypeStruct(mine.shape, F32),
        compiler_params=pltpu.CompilerParams(vmem_limit_bytes=VMEM_RESIDUAL),
        name="residual",
    )(mine, theirs, labels)


def total_kernel(*refs, scale):
    *halves, gradient, tiles = refs
    left, squares = 0, 0.0
    for mine, theirs in zip(halves[::2], halves[1::2]):
        value = (mine[...] + theirs[...]) * F32(scale)
        gradient[:, left : left + value.shape[1]] = value
        left += value.shape[1]
        squares += jnp.sum(value * value)
    tiles[...] = jnp.broadcast_to(squares, tiles.shape)


def total_call(halves, devices, scale):
    whole = pl.BlockSpec(memory_space=pltpu.VMEM)
    rows, feats = halves[0].shape[0], sum(half.shape[1] for half in halves[::2])
    return pl.pallas_call(
        functools.partial(total_kernel, scale=scale),
        in_specs=[whole] * len(halves),
        out_specs=[whole] * 2,
        out_shape=[
            jax.ShapeDtypeStruct((rows, feats), F32),
            jax.ShapeDtypeStruct((devices, 8, 128), F32),
        ],
        compiler_params=pltpu.CompilerParams(vmem_limit_bytes=VMEM_STEP),
        name="total",
    )(*halves)


def look_kernel(weights, velocity, look, look_high):
    write_look(weights[...] + F32(MOMENTUM) * velocity[...], look, look_high)


def write_look(value, look, look_high):
    classes, feats = value.shape
    rows = look_high.shape[0]
    if rows > classes:
        value = jnp.concatenate([value, jnp.zeros((rows - classes, feats), F32)], axis=0)
    high, low = split(value)
    look[...] = jnp.concatenate([high, low], axis=0)
    look_high[...] = high


def step_kernel(tiles, gradient, weights, velocity, weights_out, velocity_out, *looks, count):
    classes = weights.shape[0]
    squares = jnp.sum(tiles[...], axis=0)[:1, :1]
    rate = F32(STEP_RATE) / jnp.sqrt(squares / F32(count) + F32(EPSILON))
    velocity_now = F32(MOMENTUM) * velocity[...] - gradient[:classes] * rate
    weights_now = weights[...] + velocity_now
    velocity_out[...] = velocity_now
    weights_out[...] = weights_now
    if looks:
        write_look(weights_now + F32(MOMENTUM) * velocity_now, *looks)


def looks_of(weights):
    rows, feats = pad_rows(weights.shape[0]), weights.shape[1]
    return [jax.ShapeDtypeStruct((2 * rows, feats), BF16), jax.ShapeDtypeStruct((rows, feats), BF16)]


def look_call(weights, velocity):
    whole = pl.BlockSpec(memory_space=pltpu.VMEM)
    return pl.pallas_call(
        look_kernel,
        in_specs=[whole] * 2,
        out_specs=[whole] * 2,
        out_shape=looks_of(weights),
        compiler_params=pltpu.CompilerParams(vmem_limit_bytes=VMEM_STEP),
        name="look",
    )(weights, velocity)


def step_call(tiles, gradient, weights, velocity, count, last):
    whole = pl.BlockSpec(memory_space=pltpu.VMEM)
    out_shape = [jax.ShapeDtypeStruct(weights.shape, F32)] * 2 + ([] if last else looks_of(weights))
    return pl.pallas_call(
        functools.partial(step_kernel, count=count),
        in_specs=[whole] * 4,
        out_specs=[whole] * len(out_shape),
        out_shape=out_shape,
        compiler_params=pltpu.CompilerParams(vmem_limit_bytes=VMEM_STEP),
        name="step",
    )(tiles, gradient, weights, velocity)


def first_scores(known, proj_parts, phase_turns, look, ready, blocks, groups):
    count = lax.axis_size("feat")
    columns = known[0].shape[0]
    parts, own, others, arrived, after = [], [], [], [], [ready]
    for group in groups:
        here = [known[j] for j in blocks_in(blocks, group)]
        high, low, *sums = features_call(
            here, proj_parts, phase_turns, look, after, widths_of(group, columns), 512
        )
        parts.append((high, low))
        after = [sums[0]] + arrived
        arrived = []
        for (unit, _), value in zip(group, sums):
            if unit == 0:
                own.append(value)
            else:
                arrived.append(lax.ppermute(value, "feat", [(i, i ^ unit) for i in range(count)]))
        others += arrived
    return parts, sum(others, jnp.concatenate(own, axis=1))


def next_scores(parts, look, groups, columns):
    after, own, found = look[1], [], {}
    order = list(zip(groups, parts))
    for group, (high, low) in order[:1:-1] + order[:2]:
        sums = scores_call(look, high, low, after, widths_of(group, columns))
        after = sums[0]
        for (unit, half), value in zip(group, sums):
            found[unit, half] = value
    found[0, None] = jnp.concatenate([found.pop((0, 0)), found.pop((0, 1))], axis=1)
    bits = lax.axis_size("feat").bit_length() - 2
    return gather_sum({unit: value for (unit, _), value in found.items()}, "feat", list(range(bits)))


def on_device(frames, labels, proj, phase, class_weights, velocity):
    feat_count = lax.axis_size("feat") * proj.shape[1]
    classes = class_weights.shape[1]
    feat_scale = math.sqrt(2.0 / feat_count)
    count_all = feat_count * classes
    columns = frames.shape[0]
    bits = lax.axis_size("feat").bit_length() - 1
    blocks, groups = units_of("feat")
    me = lax.axis_index("feat")
    labels_own = jnp.concatenate(
        [lax.dynamic_slice(labels, (owner * columns,), (columns,)) for owner in (me, me ^ (1 << bits - 1))]
    )[None, :]
    known = spread(frames, "feat", list(range(bits)))
    proj_parts = split_array(proj * F32(TURN))
    phase_turns = (phase * F32(TURN))[None, :]
    weights_now = class_weights.T
    velocity_now = velocity.T
    look = look_call(weights_now, velocity_now)
    for iteration in range(ITERS):
        if iteration == 0:
            parts, mine = first_scores(known, proj_parts, phase_turns, look, labels_own, blocks, groups)
        else:
            mine = next_scores(parts, look, groups, columns)
        residual = residual_call(mine, swap(mine, "feat", bits - 1), labels_own, classes, feat_scale)
        residual = spread(residual, "feat", list(range(bits - 1)))
        gradient, halves = None, []
        for group, (high, low) in zip(groups, parts):
            here = [residual[u] for u, _ in group], [half for _, half in group], high, low
            if group is groups[-1]:
                middle = high.shape[1] // 2
                for start in (0, middle):
                    mine = gradient_call(*here, gradient, middle, start, start + middle)
                    halves += [mine, swap(mine, "frame", 0)]
            else:
                gradient = gradient_call(*here, gradient, high.shape[1] // 2)
        gradient, tiles = total_call(halves, 1 << bits, feat_scale)
        tiles = lax.all_to_all(tiles, "feat", 0, 0)
        weights_now, velocity_now, *look = step_call(
            tiles, gradient, weights_now, velocity_now, count_all, iteration == ITERS - 1
        )
    return (weights_now.T, velocity_now.T)


def solution(mesh):
    return jax.shard_map(
        on_device,
        mesh=mesh,
        in_specs=(
            P(("frame", "feat"), None),
            P("frame"),
            P(None, "feat"),
            P("feat"),
            P("feat", None),
            P("feat", None),
        ),
        out_specs=(P("feat", None), P("feat", None)),
        check_vma=False,
    )
```
